128 devices in a mesh: gx: 16 (over y, x), gy: 8 (over z, core).
Axes of the slice: x: 4, y: 4, z: 4, core: 2. Of those that a mesh axis runs over, the one named last changes fastest.
Arguments:
- coefficient: float32 [2, 2, 2, 128, 128, 128], P(None, None, None, 'gx', 'gy'), may hold values from 0.05 to 5
- owner: int32 [128, 128], P('gx', 'gy'), may hold values from 0 to 127, as said below
- w_in: bfloat16 [128, 27], replicated, may hold values from -1.25 to 1.25
- b_in: float32 [128], replicated, may hold values from -3 to 3
- w_mid: bfloat16 [2, 128, 128], replicated, may hold values from -0.5 to 0.5
- b_mid: float32 [2, 128], replicated, may hold values from -3 to 3
- w_out: bfloat16 [27, 128], replicated, may hold values from -0.5 to 0.5
- b_out: float32 [27], replicated, may hold values from -4 to 4
Outputs:
- relaid: float32 [32768, 27, 128], P(('gx', 'gy'))
The draws below stay inside these ranges and needn't reach their ends.
Inputs may be any that keep to these rules, and one draw needn't show every extreme that they name: Among the 8 x 16 columns of one device, no owner appears more than 2 times, and one owner, the same for every device, appears exactly 2 times on every device.
All inputs are finite; a program needn't handle non-finite values.
Results may differ from the reference program's by a relative error of at most 0.004.
Values sent between devices are 32-bit elements; how exact they have to be, the bound alone decides.
No kernel may reach another device: no remote copies, remote signals or barrier semaphores. Data moves between devices by JAX's collectives and lax.ppermute only.
A program may use at most 128 MiB of HBM per device.

```python
import math
import jax
import jax.numpy as jnp
from jax import lax

CX = 8
CY = 16
CZ = 128
HID = 128
MID = 2
STENCIL = 27
NCX = 128
NCY = 128
MOST = 2
N_GX = 16
N_GY = 8


def draw_owner(key, part):
    devices = N_GX * N_GY
    columns = CX * CY
    busiest = jax.random.randint(jax.random.fold_in(key, 7), (), 0, devices)

    def one_device(dev_key):
        first_key, second_key, third_key = jax.random.split(dev_key, 3)
        others = (busiest + 1 + jax.random.permutation(first_key, devices - 1)) % devices
        others_pool = jnp.repeat(others, MOST)
        others_pool = jax.random.permutation(second_key, others_pool)[:columns - MOST]
        listed = jnp.concatenate([jnp.full((MOST,), busiest, jnp.int32), others_pool.astype(jnp.int32)])
        return jax.random.permutation(third_key, listed)
    device_keys = jax.random.split(jax.random.fold_in(key, 11), devices)
    owner_table = jax.vmap(one_device)(device_keys)
    owner_table = owner_table.reshape(N_GX, N_GY, CX, CY).transpose(0, 2, 1, 3).reshape(CX * N_GX, CY * N_GY)
    return owner_table.astype(jnp.int32)


def block_levels(stream_key, shape, cuts, smallest, largest):
    gain, own = 1.0, jax.random.fold_in(stream_key, 6)
    for axis_at, parts in cuts:
        steps = jnp.exp(jax.random.uniform(jax.random.fold_in(own, axis_at), (parts,), jnp.float32, smallest / len(cuts), largest / len(cuts)))
        gain = gain * jnp.repeat(steps, shape[axis_at] // parts).reshape([-1 if axis == axis_at else 1 for axis in range(len(shape))])
    return gain


def normal_values(stream_key, dims, width, limit, kind=jnp.bfloat16):
    drawn = jax.random.normal(stream_key, dims, jnp.float32) * width
    return jnp.minimum(jnp.maximum(drawn, -limit), limit).astype(kind)


def setup_inputs(seed: int = 0) -> dict:
    splits = jax.random.split(jax.random.key(seed), 9)
    return {
        "coefficient": jnp.clip(jnp.exp(math.log(5.0) - 4.6051702 * jax.random.uniform(splits[0], (2, 2, 2, NCX, NCY, CZ), jnp.float32) ** block_levels(splits[0], (2, 2, 2, NCX, NCY, CZ), ((3, 16), (4, 8)), -0.2, 0.2)), 0.05, 5.0),
        "owner": draw_owner(jax.random.fold_in(splits[8], 71), 0),
        "w_in": jnp.clip(jax.random.uniform(splits[2], (HID, STENCIL), jnp.float32, -1.25, 1.25), -1.25, 1.25).astype(jnp.bfloat16),
        "b_in": normal_values(splits[3], (HID,), 0.5, 3.0, jnp.float32),
        "w_mid": normal_values(splits[4], (MID, HID, HID), HID ** -0.5, 0.5),
        "b_mid": normal_values(splits[5], (MID, HID), 0.5, 3.0, jnp.float32),
        "w_out": jnp.clip(jax.random.uniform(splits[6], (STENCIL, HID), jnp.float32, -0.5, 0.5), -0.5, 0.5).astype(jnp.bfloat16),
        "b_out": normal_values(splits[7], (STENCIL,), 1.0, 4.0, jnp.float32),
    }


def offset_list():
    return [(shift_x, shift_y, shift_z) for shift_x in (-1, 0, 1) for shift_y in (-1, 0, 1) for shift_z in (-1, 0, 1)]

def parity_key(offset):
    return tuple((0 if component == 0 else 1 for component in offset))

def shift_next(values, which_axis):
    length = values.shape[which_axis]
    upper_part = lax.slice_in_dim(values, 1, length, axis=which_axis)
    filler = jnp.zeros_like(lax.slice_in_dim(values, 0, 1, axis=which_axis))
    return jnp.concatenate([upper_part, filler], axis=which_axis)

def shift_prev(values, which_axis):
    length = values.shape[which_axis]
    lower_part = lax.slice_in_dim(values, 0, length - 1, axis=which_axis)
    filler = jnp.zeros_like(lax.slice_in_dim(values, 0, 1, axis=which_axis))
    return jnp.concatenate([filler, lower_part], axis=which_axis)

def gather_offsets(fine_field):
    fields = []
    for offset in offset_list():
        portion = fine_field[parity_key(offset)]
        for which_axis, component in enumerate(offset):
            if component == -1:
                portion = shift_prev(portion, which_axis)
        fields.append(portion)
    return fields

def restrict(fine_field, weights):
    fields = gather_offsets(fine_field)
    accumulated = weights[0] * fields[0]
    for index_o in range(1, len(fields)):
        accumulated = accumulated + weights[index_o] * fields[index_o]
    return accumulated

def prolong(weights):
    parity_sums = {}
    for index_o, offset in enumerate(offset_list()):
        portion = weights[index_o]
        for which_axis, component in enumerate(offset):
            if component == -1:
                portion = shift_next(portion, which_axis)
        target = parity_key(offset)
        if target in parity_sums:
            parity_sums[target] = parity_sums[target] + portion
        else:
            parity_sums[target] = portion
    return jnp.stack([jnp.stack([jnp.stack([parity_sums[parity_x, parity_y, parity_z] for parity_z in (0, 1)]) for parity_y in (0, 1)]) for parity_x in (0, 1)])

def step_plus(values, which_axis):
    even_part = lax.slice_in_dim(values, 0, 1, axis=which_axis)
    odd_part = lax.slice_in_dim(values, 1, 2, axis=which_axis)
    return jnp.concatenate([odd_part, shift_next(even_part, which_axis + 3)], axis=which_axis)

def step_minus(values, which_axis):
    even_part = lax.slice_in_dim(values, 0, 1, axis=which_axis)
    odd_part = lax.slice_in_dim(values, 1, 2, axis=which_axis)
    return jnp.concatenate([shift_prev(odd_part, which_axis + 3), even_part], axis=which_axis)

def operate(field, face_coef):
    accumulated = jnp.zeros_like(field)
    for which_axis in range(3):
        face = face_coef[which_axis]
        accumulated = accumulated + face * (field - step_plus(field, which_axis))
        accumulated = accumulated + step_minus(face, which_axis) * (field - step_minus(field, which_axis))
    return accumulated

def pick_offsets(probe_stack):
    for which_axis in range(3):
        grid_shape = [1] * probe_stack.ndim
        grid_shape[which_axis + 3] = probe_stack.shape[which_axis + 3]
        position = lax.broadcasted_iota(jnp.int32, tuple(grid_shape), which_axis + 3)
        picked_rows = []
        for offset in (-1, 0, 1):
            wanted = (position + offset + 3) % 3
            chosen = jnp.zeros_like(lax.slice_in_dim(probe_stack, 0, 1, axis=which_axis))
            for probe_class in range(3):
                chosen = chosen + jnp.where(wanted == probe_class, lax.slice_in_dim(probe_stack, probe_class, probe_class + 1, axis=which_axis), 0.0)
            picked_rows.append(chosen)
        probe_stack = jnp.concatenate(picked_rows, axis=which_axis)
    return probe_stack

def galerkin(weights_ext, kappa_ext):
    face_coef = [jnp.sqrt(kappa_ext * step_plus(kappa_ext, which_axis)) for which_axis in range(3)]
    grid_shape = weights_ext.shape[1:]
    place_x = lax.broadcasted_iota(jnp.int32, grid_shape, 0) % 3
    place_y = lax.broadcasted_iota(jnp.int32, grid_shape, 1) % 3
    place_z = lax.broadcasted_iota(jnp.int32, grid_shape, 2) % 3

    def probe(probe_class, probe_stack):
        chosen = (place_x == probe_class // 9) & (place_y == probe_class // 3 % 3) & (place_z == probe_class % 3)
        masked = jnp.where(chosen[None], weights_ext, 0.0)
        applied = operate(prolong(masked), face_coef)
        return lax.dynamic_update_index_in_dim(probe_stack, restrict(applied, weights_ext), probe_class, 0)
    probe_stack = lax.fori_loop(0, 27, probe, jnp.zeros(weights_ext.shape, jnp.float32))
    picked = pick_offsets(probe_stack.reshape((3, 3, 3) + grid_shape)).reshape(weights_ext.shape)
    return picked[:, 1:-1, 1:-1, 1:-1]

def predict(feature_rows, w_in, b_in, w_mid, b_mid, w_out, b_out):
    hidden = jax.nn.silu(jnp.dot(w_in, feature_rows, preferred_element_type=jnp.float32) + b_in[:, None]).astype(jnp.bfloat16)
    for layer_num in range(w_mid.shape[0]):
        hidden = jax.nn.silu(jnp.dot(w_mid[layer_num], hidden, preferred_element_type=jnp.float32) + b_mid[layer_num][:, None]).astype(jnp.bfloat16)
    return 0.5 * jax.nn.sigmoid(jnp.dot(w_out, hidden, preferred_element_type=jnp.float32) + b_out[:, None])

def reference(coefficient, owner, w_in, b_in, w_mid, b_mid, w_out, b_out):
    kappa_ext = jnp.pad(coefficient, ((0, 0), (0, 0), (0, 0), (1, 1), (1, 1), (1, 1)))
    raw_features = jnp.stack(gather_offsets(jnp.log1p(kappa_ext)))[:, 1:-1, 1:-1, 1:-1]
    feature_grid = raw_features.astype(jnp.bfloat16)

    def per_slab(slab_cells):
        flat_cells = slab_cells.reshape(slab_cells.shape[0], -1)
        return predict(flat_cells, w_in, b_in, w_mid, b_mid, w_out, b_out).reshape(slab_cells.shape)
    weights = jnp.moveaxis(lax.map(per_slab, jnp.moveaxis(feature_grid, 1, 0)), 0, 1)
    weights_ext = jnp.pad(weights, ((0, 0), (1, 1), (1, 1), (1, 1)))
    stencil = galerkin(weights_ext, kappa_ext)
    devices = N_GX * N_GY
    columns = CX * CY
    blocks = stencil.reshape(STENCIL, N_GX, CX, N_GY, CY, CZ).transpose(1, 3, 2, 4, 0, 5).reshape(devices * columns, STENCIL, CZ)
    owners = owner.reshape(N_GX, CX, N_GY, CY).transpose(0, 2, 1, 3).reshape(devices, columns)
    matches = (owners[:, :, None] == jnp.arange(devices, dtype=jnp.int32)[None, None, :]).astype(jnp.int32)
    order_rank = lax.optimization_barrier(jnp.sum(jnp.cumsum(matches, axis=1) * matches, axis=2)) - 1
    source = jnp.arange(devices, dtype=jnp.int32)[:, None]
    slot_index = (owners * (devices * MOST) + source * MOST + order_rank).reshape(-1).astype(jnp.int32)
    relaid = jnp.zeros((devices * devices * MOST, STENCIL, CZ), jnp.float32).at[slot_index].set(blocks)
    return relaid
```

```python
import functools

import jax
import jax.numpy as jnp
import numpy as np
from jax import lax
from jax.experimental import pallas as pl
from jax.experimental.pallas import tpu as pltpu
from jax.sharding import PartitionSpec as P

OFFSETS = [(a, b, c) for a in (-1, 0, 1) for b in (-1, 0, 1) for c in (-1, 0, 1)]
INNER = 27
PITCH = 28
YP = 32
Y0 = 8


def parity(o):
    return 4 * (o[0] != 0) + 2 * (o[1] != 0) + (o[2] != 0)


def tile_row(o):
    return 32 * (o[0] == -1) + 16 * (o[1] == -1) + 8 * (o[2] == -1) + parity(o)


def spread():
    m = np.zeros((27, 64), np.float32)
    for n, o in enumerate(OFFSETS):
        m[n, tile_row(o)] = 1.0
    return m


def z_before(v):
    lane = lax.broadcasted_iota(jnp.int32, v.shape, v.ndim - 1)
    return jnp.where(lane == 0, 0.0, pltpu.roll(v, 1, v.ndim - 1))


def z_after(v):
    lane = lax.broadcasted_iota(jnp.int32, v.shape, v.ndim - 1)
    last = v.shape[-1] - 1
    return jnp.where(lane == last, 0.0, pltpu.roll(v, last, v.ndim - 1))


def main_kernel(nx, ny, edge_ref, owner_ref, coef_ref, xlo_ref, xhi_ref, ylo_ref, yhi_ref,
                w1_ref, b1_ref, wm_ref, bm_ref, wo_ref, bo_ref, out_ref,
                k_ref, r_ref, f_ref, rt_ref, t_ref, u_ref, s_ref, count_ref):
    nz = 128
    ex, ey = nx + 3, ny + 3
    hx, hy = nx + 2, ny + 2
    kp = ex * YP
    up = hx * hy
    for p in range(8):
        k_ref[p, 2:2 + nx, Y0:Y0 + ny] = coef_ref[p]
        k_ref[p, 0:2, Y0:Y0 + ny] = xlo_ref[p]
        k_ref[p, 2 + nx:, Y0:Y0 + ny] = xhi_ref[p]
        for x in range(ex):
            k_ref[p, x, Y0 - 2:Y0] = ylo_ref[p, x]
            k_ref[p, x, Y0 + ny:Y0 + ny + 1] = yhi_ref[p, x]
    flat_k = k_ref.reshape(8 * kp, nz)
    flat_r = r_ref.reshape(8 * kp, nz)

    def roots(i, _):
        rows = pl.ds(pl.multiple_of(i * YP, YP), YP)
        flat_r[rows, :] = jnp.sqrt(flat_k[rows, :])
        return _

    lax.fori_loop(0, 8 * ex, roots, 0)

    def tiles(x, _):
        for y in range(ey):
            kt = flat_k[pl.ds(x * YP + Y0 - 2 + y, 8, stride=kp), :]
            logs = jnp.log(1.0 + kt)
            f_ref[x, y] = jnp.concatenate([logs, z_before(logs)], 0).astype(jnp.bfloat16)
            rt = jnp.sqrt(kt)
            rt_ref[x, y, 0:8] = rt
            rt_ref[x, y, 8:16] = z_before(rt)
        return _

    lax.fori_loop(0, ex, tiles, 0)

    def ratios(x, _):
        for blk in range(0, ny + 1, 8):
            rows = min(8, ny + 1 - blk)

            def at(px, py, pz, dx, dy):
                p = 4 * px + 2 * py + pz
                return flat_r[pl.ds(p * kp + (x + 1 + dx) * YP + Y0 - 1 + blk + dy, rows), :]

            for p in range(8):
                px, py, pz = p >> 2, (p >> 1) & 1, p & 1
                own = at(px, py, pz, 0, 0)
                total = at(1 - px, py, pz, 0, 0) + at(1 - px, py, pz, 1 if px else -1, 0)
                total += at(px, 1 - py, pz, 0, 0) + at(px, 1 - py, pz, 0, 1 if py else -1)
                beside = at(px, py, 1 - pz, 0, 0)
                total += beside + (z_after(beside) if pz else z_before(beside))
                t = jnp.where(own > 0.0, total / jnp.where(own > 0.0, own, 1.0), 0.0)
                t_ref[p, x, pl.ds(blk, rows), :] = t
                if pz:
                    t_ref[8 + p // 2, x, pl.ds(blk, rows), :] = z_before(t)
        return _

    lax.fori_loop(0, nx + 1, ratios, 0)

    group = 6

    def predict(x, _):
        for y0 in range(0, hy, group):
            parts = []
            for y in range(y0, y0 + group):
                parts.append(jnp.concatenate(
                    [f_ref[x + 1, y + 1], f_ref[x + 1, y], f_ref[x, y + 1], f_ref[x, y]], 0))
            h = jnp.concatenate(parts, 1)
            v = jnp.dot(w1_ref[...], h, preferred_element_type=jnp.float32) + b1_ref[...]
            h = (v + v * jnp.tanh(v)).astype(jnp.bfloat16)
            for m in range(2):
                v = jnp.dot(wm_ref[m], h, preferred_element_type=jnp.float32) + bm_ref[m]
                h = (v + v * jnp.tanh(v)).astype(jnp.bfloat16)
            v = jnp.dot(wo_ref[...], h, preferred_element_type=jnp.float32) + bo_ref[...]
            w = 0.25 + 0.25 * jnp.tanh(v)
            for y in range(y0, y0 + group):
                inside = jnp.logical_not(
                    jnp.logical_or(jnp.logical_and(x == hx - 1, edge_ref[0] == 1),
                                   jnp.logical_and(y == hy - 1, edge_ref[1] == 1)))
                keep = jnp.where(inside, 1.0, 0.0)
                wy = w[:, (y - y0) * nz:(y - y0 + 1) * nz] * keep
                for q, (sx, sy) in enumerate(((0, 0), (0, 1), (1, 0), (1, 1))):
                    for sz in range(2):
                        part = 16 * q + 8 * sz
                        u = wy[part:part + 8] * rt_ref[x + 1 - sx, y + 1 - sy, 8 * sz:8 * sz + 8]
                        at = part * up + x * hy + y
                        u_ref[0, pl.ds(at, 8, stride=up), :] = u
                        u_ref[1, pl.ds(at, 8, stride=up), :] = z_after(u)
                        if not sz:
                            u_ref[2, pl.ds(at, 8, stride=up), :] = z_before(u)
        return _

    lax.fori_loop(0, hx, predict, 0)

    def galerkin(x, _):
        for yb in range(0, ny, 8):

            def u_at(f, o):
                plane = tile_row(f)
                which = {0: 0, 1: 1, -1: 2}[o[2]]
                row = plane * up + (x + 1 + o[0]) * hy + yb + 1 + o[1]
                return u_ref[which, pl.ds(row, 8), :]

            own = {f: u_at(f, (0, 0, 0)) for f in OFFSETS}
            q = {}
            for f in OFFSETS:
                p = parity(f)
                plane = 8 + p // 2 if f[2] == -1 else p
                t = t_ref[plane, x + 1 - (f[0] == -1), pl.ds(yb + 1 - (f[1] == -1), 8), :]
                total = t * own[f]
                for d in range(3):
                    for step in (-1, 1):
                        g = tuple(f[n] + (step if n == d else 0) for n in range(3))
                        if g in own:
                            total = total - own[g]
                q[f] = total
            for n, o in enumerate(OFFSETS):
                plus = minus = None
                for fx in range(-2, 3):
                    for fy in range(-2, 3):
                        for fz in range(-2, 3):
                            f = (fx, fy, fz)
                            far = [d for d in range(3) if abs(f[d]) == 2]
                            g = tuple(f[d] - 2 * o[d] for d in range(3))
                            if len(far) > 1 or max(map(abs, g)) > 1:
                                continue
                            other = u_at(g, o)
                            if far:
                                near = tuple(v // 2 if d == far[0] else v for d, v in enumerate(f))
                                term = other * own[near]
                                minus = term if minus is None else minus + term
                            else:
                                term = other * q[f]
                                plus = term if plus is None else plus + term
                total = plus if minus is None else plus - minus
                s_ref[pl.ds(n * nx * ny + x * ny + yb, 8), :] = total
        return _

    lax.fori_loop(0, nx, galerkin, 0)

    def clear(i, _):
        out_ref[pl.ds(pl.multiple_of(i * 56, 8), 56), :] = jnp.zeros((56, nz), jnp.float32)
        count_ref[i] = 0
        return _

    lax.fori_loop(0, out_ref.shape[0] // 56, clear, 0)

    def place(x, _):
        for y in range(ny):
            who = owner_ref[x, y]
            rank = count_ref[who]
            count_ref[who] = rank + 1
            row = (who * 2 + rank) * PITCH
            c = x * ny + y
            for n in (0, 8, 16, 24):
                size = min(8, INNER - n)
                out_ref[pl.ds(row + n, size), :] = s_ref[pl.ds(n * nx * ny + c, size, stride=nx * ny), :]
        return _

    lax.fori_loop(0, nx, place, 0)


def unpack_kernel(in_ref, out_ref):
    slots = out_ref.shape[1]

    def one(o, _):
        for k in range(0, slots, 8):
            out_ref[o, pl.ds(k, 8), :] = in_ref[pl.ds(k * PITCH + o, 8, stride=PITCH), :]
        return _

    lax.fori_loop(0, out_ref.shape[0], one, 0)


def per_device(coefficient, owner, w_in, b_in, w_mid, b_mid, w_out, b_out):
    nx, ny, nz = coefficient.shape[3:]
    devices = lax.axis_size("gx") * lax.axis_size("gy")
    k = coefficient.reshape(8, nx, ny, nz)

    def send(v, axis, step):
        size = lax.axis_size(axis)
        pairs = [(i, i + step) for i in range(size) if 0 <= i + step < size]
        return lax.ppermute(v, axis, pairs)

    xlo = send(k[:, nx - 2:], "gx", 1)
    xhi = send(k[:, :1], "gx", -1)
    kx = lambda a, b: jnp.concatenate([xlo[:, :, a:b], k[:, :, a:b], xhi[:, :, a:b]], 1)
    ylo = send(kx(ny - 2, ny), "gy", 1)
    yhi = send(kx(0, 1), "gy", -1)

    spread_rows = jnp.asarray(spread(), jnp.bfloat16)
    w1 = jnp.dot(w_in * jnp.bfloat16(0.5), spread_rows, preferred_element_type=jnp.float32).astype(jnp.bfloat16)
    wo = jnp.dot(spread_rows.T, w_out * jnp.bfloat16(0.5), preferred_element_type=jnp.float32).astype(jnp.bfloat16)
    bo = jnp.dot(jnp.asarray(spread().T), b_out * 0.5, precision=lax.Precision.HIGHEST)
    edge = jnp.stack([lax.axis_index("gx") == lax.axis_size("gx") - 1,
                      lax.axis_index("gy") == lax.axis_size("gy") - 1]).astype(jnp.int32)
    ex, ey, hx, hy = nx + 3, ny + 3, nx + 2, ny + 2
    vmem = pl.BlockSpec(memory_space=pltpu.VMEM)
    smem = pl.BlockSpec(memory_space=pltpu.SMEM)
    out = pl.pallas_call(
        functools.partial(main_kernel, nx, ny),
        out_shape=jax.ShapeDtypeStruct((devices * 2 * PITCH, nz), jnp.float32),
        in_specs=[smem, smem] + [vmem] * 11,
        out_specs=vmem,
        scratch_shapes=[
            pltpu.VMEM((8, ex, YP, nz), jnp.float32),
            pltpu.VMEM((8, ex, YP, nz), jnp.float32),
            pltpu.VMEM((ex, ey, 16, nz), jnp.bfloat16),
            pltpu.VMEM((ex, ey, 16, nz), jnp.float32),
            pltpu.VMEM((12, nx + 1, 24, nz), jnp.float32),
            pltpu.VMEM((3, 64 * hx * hy, nz), jnp.float32),
            pltpu.VMEM((INNER * nx * ny, nz), jnp.float32),
            pltpu.SMEM((devices,), jnp.int32),
        ],
        compiler_params=pltpu.CompilerParams(vmem_limit_bytes=48 * 2**20),
        name="stencils",
    )(edge, owner, k, xlo, xhi, ylo, yhi, w1, b_in[:, None] * 0.5, w_mid * jnp.bfloat16(0.5),
      b_mid[:, :, None] * 0.5, wo, bo[:, None])
    got = lax.all_to_all(out.reshape(devices, 2 * PITCH, nz), ("gx", "gy"), split_axis=0, concat_axis=0, tiled=True)
    relaid = pl.pallas_call(
        unpack_kernel,
        out_shape=jax.ShapeDtypeStruct((27, devices * 2, nz), jnp.float32),
        in_specs=[vmem],
        out_specs=vmem,
        compiler_params=pltpu.CompilerParams(vmem_limit_bytes=32 * 2**20),
        name="unpack",
    )(got.reshape(devices * 2 * PITCH, nz))
    return jnp.transpose(relaid, (1, 0, 2))


def solution(mesh):
    return jax.shard_map(
        per_device,
        mesh=mesh,
        in_specs=(P(None, None, None, "gx", "gy", None), P("gx", "gy"), P(), P(), P(), P(), P(), P()),
        out_specs=P(("gx", "gy"), None, None),
        check_vma=False,
    )
```

```python
import functools

import jax
import jax.numpy as jnp
from jax import lax
from jax.experimental import pallas as pl
from jax.experimental.pallas import tpu as pltpu
from jax.sharding import PartitionSpec as P

OFFSETS = [(a, b, c) for a in (-1, 0, 1) for b in (-1, 0, 1) for c in (-1, 0, 1)]
SENT = [o for o in OFFSETS if o != (0, 0, -1)]
PITCH = len(SENT)
YP = 32
Y0 = 8


def parity(o):
    return 4 * (o[0] != 0) + 2 * (o[1] != 0) + (o[2] != 0)


def tile_row(o):
    return 32 * (o[0] == -1) + 16 * (o[1] == -1) + 8 * (o[2] == -1) + parity(o)


def offset_of_row(shape, dim):
    row = lax.broadcasted_iota(jnp.int32, shape, dim)
    number = jnp.zeros(shape, jnp.int32)
    none = jnp.zeros(shape, jnp.bool_)
    for lower, odd, scale in ((5, 2, 9), (4, 1, 3), (3, 0, 1)):
        low, away = (row >> lower) & 1, (row >> odd) & 1
        number += (1 + away - 2 * low) * scale
        none = jnp.logical_or(none, low > away)
    return jnp.where(none, -1, number)


def as_column(row, chosen):
    return jnp.sum(jnp.where(chosen, row, 0.0), axis=1, keepdims=True)


def z_before(v):
    lane = lax.broadcasted_iota(jnp.int32, v.shape, v.ndim - 1)
    return jnp.where(lane == 0, 0.0, pltpu.roll(v, 1, v.ndim - 1))


def z_after(v):
    lane = lax.broadcasted_iota(jnp.int32, v.shape, v.ndim - 1)
    last = v.shape[-1] - 1
    return jnp.where(lane == last, 0.0, pltpu.roll(v, last, v.ndim - 1))


def send_x_kernel(k_ref, up_ref, down_ref):
    nx = k_ref.shape[1]
    up_ref[...] = k_ref[:, nx - 2:]
    down_ref[...] = k_ref[:, :1]


def send_y_kernel(k_ref, xlo_ref, xhi_ref, up_ref, down_ref):
    nx, ny = k_ref.shape[1:3]
    for to, rows in ((up_ref, slice(ny - 2, ny)), (down_ref, slice(0, 1))):
        to[:, 0:2] = xlo_ref[:, :, rows]
        to[:, 2:2 + nx] = k_ref[:, :, rows]
        to[:, 2 + nx:] = xhi_ref[:, :, rows]


def feature_tile(kt):
    logs = jnp.log(1.0 + kt)
    return jnp.concatenate([logs, z_before(logs)], 0).astype(jnp.bfloat16)


def mlp(f, columns, layers):
    w1_ref, b1_ref, wm_ref, bm_ref, wo_ref, bo_ref = layers
    h = jnp.concatenate(
        [jnp.concatenate([f(x, y), f(x, y - 1), f(x - 1, y), f(x - 1, y - 1)], 0) for x, y in columns], 1)
    v = jnp.dot(w1_ref[...], h, preferred_element_type=jnp.float32) + b1_ref[...]
    h = (v + v * jnp.tanh(v)).astype(jnp.bfloat16)
    for m in range(2):
        v = jnp.dot(wm_ref[m], h, preferred_element_type=jnp.float32) + bm_ref[m]
        h = (v + v * jnp.tanh(v)).astype(jnp.bfloat16)
    v = jnp.dot(wo_ref[...], h, preferred_element_type=jnp.float32) + bo_ref[...]
    return 0.25 + 0.25 * jnp.tanh(v)


def inner_kernel(nx, ny, k_ref, win_ref, bin_ref, wmid_ref, bmid_ref, wout_ref, bout_ref,
                 w1_ref, b1_ref, wm_ref, bm_ref, wo_ref, bo_ref, w_ref, f_ref):
    nz = 128
    half = jnp.bfloat16(0.5)
    eye = lax.broadcasted_iota(jnp.int32, (128, 128), 0) == lax.broadcasted_iota(jnp.int32, (128, 128), 1)
    into = offset_of_row((27, 64), 1) == lax.broadcasted_iota(jnp.int32, (27, 64), 0)
    out_of = offset_of_row((64, 27), 0) == lax.broadcasted_iota(jnp.int32, (64, 27), 1)
    ones = lambda m: jnp.where(m, 1.0, 0.0).astype(jnp.bfloat16)
    w1_ref[...] = jnp.dot(win_ref[...] * half, ones(into), preferred_element_type=jnp.float32).astype(jnp.bfloat16)
    wo_ref[...] = jnp.dot(ones(out_of), wout_ref[...] * half, preferred_element_type=jnp.float32).astype(jnp.bfloat16)
    b1_ref[...] = as_column(bin_ref[...], eye) * 0.5
    bo_ref[...] = as_column(bout_ref[...], out_of) * 0.5
    for m in range(2):
        wm_ref[m] = wmid_ref[m] * half
        bm_ref[m] = as_column(bmid_ref[m:m + 1], eye) * 0.5
    layers = (w1_ref, b1_ref, wm_ref, bm_ref, wo_ref, bo_ref)
    flat = k_ref.reshape(8 * nx * ny, nz)

    def tiles(x, _):
        for y in range(ny):
            f_ref[x, y] = feature_tile(flat[pl.ds(x * ny + y, 8, stride=nx * ny), :])
        return _

    lax.fori_loop(0, nx, tiles, 0)

    def row(x, _):
        w = mlp(lambda a, b: f_ref[a, b], [(x, y) for y in range(1, ny)], layers)
        for y in range(1, ny):
            w_ref[(x - 1) * (ny - 1) + y - 1] = w[:, (y - 1) * nz:y * nz]
        return _

    lax.fori_loop(1, nx, row, 0)


def side_kernel(nx, ny, k_ref, xlo_ref, xhi_ref, w1_ref, b1_ref, wm_ref, bm_ref, wo_ref, bo_ref, w_ref, k5_ref, f_ref):
    nz = 128
    layers = (w1_ref, b1_ref, wm_ref, bm_ref, wo_ref, bo_ref)
    k5_ref[:, 0:2] = xlo_ref[...]
    k5_ref[:, 2:3] = k_ref[:, 0:1]
    k5_ref[:, 3:4] = k_ref[:, nx - 1:]
    k5_ref[:, 4:5] = xhi_ref[...]
    flat = k5_ref.reshape(8 * 5 * ny, nz)

    def tiles(x, _):
        for y in range(ny):
            f_ref[x, y] = feature_tile(flat[pl.ds(x * ny + y, 8, stride=5 * ny), :])
        return _

    lax.fori_loop(0, 5, tiles, 0)

    def row(i, _):
        x = jnp.where(i == 2, 4, i + 1)
        w = mlp(lambda a, b: f_ref[a, b], [(x, y) for y in range(1, ny)], layers)
        for y in range(1, ny):
            w_ref[i * (ny - 1) + y - 1] = w[:, (y - 1) * nz:y * nz]
        return _

    lax.fori_loop(0, 3, row, 0)


def main_kernel(nx, ny, owner_ref, coef_ref, xlo_ref, xhi_ref, ylo_ref, yhi_ref,
                w1_ref, b1_ref, wm_ref, bm_ref, wo_ref, bo_ref, inner_ref, side_ref, out_ref,
                k_ref, r_ref, f_ref, rt_ref, t_ref, u_ref, s_ref, count_ref):
    nz = 128
    layers = (w1_ref, b1_ref, wm_ref, bm_ref, wo_ref, bo_ref)
    ex, ey = nx + 3, ny + 3
    hx, hy = nx + 2, ny + 2
    kp = ex * YP
    up = hx * hy
    last_x = lax.axis_index("gx") == lax.axis_size("gx") - 1
    last_y = lax.axis_index("gy") == lax.axis_size("gy") - 1

    for p in range(8):
        k_ref[p, 2:2 + nx, Y0:Y0 + ny] = coef_ref[p]
        k_ref[p, 0:2, Y0:Y0 + ny] = xlo_ref[p]
        k_ref[p, 2 + nx:, Y0:Y0 + ny] = xhi_ref[p]
        for x in range(ex):
            k_ref[p, x, Y0 - 2:Y0] = ylo_ref[p, x]
            k_ref[p, x, Y0 + ny:Y0 + ny + 1] = yhi_ref[p, x]
    flat_k = k_ref.reshape(8 * kp, nz)
    flat_r = r_ref.reshape(8 * kp, nz)

    def roots(i, _):
        rows = pl.ds(pl.multiple_of(i * YP, YP), YP)
        flat_r[rows, :] = jnp.sqrt(flat_k[rows, :])
        return _

    lax.fori_loop(0, 8 * ex, roots, 0)

    rim = {0: 0, 1: 1, 2: 2, ey - 2: 3, ey - 1: 4}

    def tiles(x, _):
        for y in range(ey):
            at = pl.ds(x * YP + Y0 - 2 + y, 8, stride=kp)
            if y in rim:
                f_ref[x, rim[y]] = feature_tile(flat_k[at, :])
            rt = flat_r[at, :]
            rt_ref[x, y, 0:8] = rt
            rt_ref[x, y, 8:16] = z_before(rt)
        return _

    lax.fori_loop(0, ex, tiles, 0)

    def ratios(x, _):
        for blk in range(0, ny + 1, 8):
            rows = min(8, ny + 1 - blk)

            def at(px, py, pz, dx, dy):
                p = 4 * px + 2 * py + pz
                return flat_r[pl.ds(p * kp + (x + 1 + dx) * YP + Y0 - 1 + blk + dy, rows), :]

            for p in range(8):
                px, py, pz = p >> 2, (p >> 1) & 1, p & 1
                own = at(px, py, pz, 0, 0)
                total = at(1 - px, py, pz, 0, 0) + at(1 - px, py, pz, 1 if px else -1, 0)
                total += at(px, 1 - py, pz, 0, 0) + at(px, 1 - py, pz, 0, 1 if py else -1)
                beside = at(px, py, 1 - pz, 0, 0)
                total += beside + (z_after(beside) if pz else z_before(beside))
                t = jnp.where(own > 0.0, total / jnp.where(own > 0.0, own, 1.0), 0.0)
                t_ref[p, x, pl.ds(blk, rows), :] = t
                if pz:
                    t_ref[8 + p // 2, x, pl.ds(blk, rows), :] = z_before(t)
        return _

    lax.fori_loop(0, nx + 1, ratios, 0)

    def put(x, y, wy):
        for q, (sx, sy) in enumerate(((0, 0), (0, 1), (1, 0), (1, 1))):
            for sz in range(2):
                part = 16 * q + 8 * sz
                u = wy[part:part + 8] * rt_ref[x + 1 - sx, y + 1 - sy, 8 * sz:8 * sz + 8]
                at = part * up + x * hy + y
                u_ref[0, pl.ds(at, 8, stride=up), :] = u
                u_ref[1, pl.ds(at, 8, stride=up), :] = z_after(u)
                if not sz:
                    u_ref[2, pl.ds(at, 8, stride=up), :] = z_before(u)

    def put_inner(x, _):
        for y in range(1, ny):
            put(x + 1, y + 1, inner_ref[(x - 1) * (ny - 1) + y - 1])
        return _

    lax.fori_loop(1, nx, put_inner, 0)

    def put_side(i, _):
        keep = jnp.where(jnp.logical_and(i == 2, last_x), 0.0, 1.0)
        for y in range(1, ny):
            put(jnp.where(i == 2, hx - 1, i), y + 1, side_ref[i * (ny - 1) + y - 1] * keep)
        return _

    lax.fori_loop(0, 3, put_side, 0)
    columns = [(x, y) for y in (0, 1, hy - 1) for x in range(hx)]
    w = mlp(lambda x, y: f_ref[x, rim[y]], [(x + 1, y + 1) for x, y in columns], layers)
    for n, (x, y) in enumerate(columns):
        wy = w[:, n * nz:(n + 1) * nz]
        if x == hx - 1:
            wy = wy * jnp.where(last_x, 0.0, 1.0)
        if y == hy - 1:
            wy = wy * jnp.where(last_y, 0.0, 1.0)
        put(x, y, wy)

    def galerkin(x, _):
        for yb in range(0, ny, 8):

            def u_at(f, o):
                plane = tile_row(f)
                which = {0: 0, 1: 1, -1: 2}[o[2]]
                row = plane * up + (x + 1 + o[0]) * hy + yb + 1 + o[1]
                return u_ref[which, pl.ds(row, 8), :]

            own = {f: u_at(f, (0, 0, 0)) for f in OFFSETS}
            q = {}
            for f in OFFSETS:
                p = parity(f)
                plane = 8 + p // 2 if f[2] == -1 else p
                t = t_ref[plane, x + 1 - (f[0] == -1), pl.ds(yb + 1 - (f[1] == -1), 8), :]
                total = t * own[f]
                for d in range(3):
                    for step in (-1, 1):
                        g = tuple(f[n] + (step if n == d else 0) for n in range(3))
                        if g in own:
                            total = total - own[g]
                q[f] = total
            for n, o in enumerate(SENT):
                plus = minus = None
                for fx in range(-2, 3):
                    for fy in range(-2, 3):
                        for fz in range(-2, 3):
                            f = (fx, fy, fz)
                            far = [d for d in range(3) if abs(f[d]) == 2]
                            g = tuple(f[d] - 2 * o[d] for d in range(3))
                            if len(far) > 1 or max(map(abs, g)) > 1:
                                continue
                            other = u_at(g, o)
                            if far:
                                near = tuple(v // 2 if d == far[0] else v for d, v in enumerate(f))
                                term = other * own[near]
                                minus = term if minus is None else minus + term
                            else:
                                term = other * q[f]
                                plus = term if plus is None else plus + term
                total = plus if minus is None else plus - minus
                s_ref[pl.ds(n * nx * ny + x * ny + yb, 8), :] = total
        return _

    lax.fori_loop(0, nx, galerkin, 0)

    def clear(i, _):
        rows = 2 * 2 * PITCH
        out_ref[pl.ds(pl.multiple_of(i * rows, 8), rows), :] = jnp.zeros((rows, nz), jnp.float32)
        count_ref[2 * i] = 0
        count_ref[2 * i + 1] = 0
        return _

    lax.fori_loop(0, out_ref.shape[0] // (2 * 2 * PITCH), clear, 0)

    def place(x, _):
        for y in range(ny):
            who = owner_ref[x, y]
            rank = count_ref[who]
            count_ref[who] = rank + 1
            row = (who * 2 + rank) * PITCH
            c = x * ny + y
            for n in (0, 8, 16, 24):
                size = min(8, PITCH - n)
                out_ref[pl.ds(row + n, size), :] = s_ref[pl.ds(n * nx * ny + c, size, stride=nx * ny), :]
        return _

    lax.fori_loop(0, nx, place, 0)


def unpack_kernel(in_ref, out_ref):
    group, slots = out_ref.shape[:2]
    below, above = OFFSETS.index((0, 0, -1)), SENT.index((0, 0, 1))
    first = pl.program_id(0) * group

    def one(i, _):
        o = first + i
        n = jnp.where(o > below, o - 1, o)
        for k in range(0, slots, 8):
            out_ref[i, pl.ds(k, 8), :] = in_ref[pl.ds(k * PITCH + n, 8, stride=PITCH), :]
        return _

    lax.fori_loop(0, group, one, 0)

    @pl.when(pl.program_id(0) == below // group)
    def _():
        for k in range(0, slots, 8):
            out_ref[below % group, pl.ds(k, 8), :] = z_before(in_ref[pl.ds(k * PITCH + above, 8, stride=PITCH), :])


def per_device(coefficient, owner, w_in, b_in, w_mid, b_mid, w_out, b_out):
    nx, ny, nz = coefficient.shape[3:]
    devices = lax.axis_size("gx") * lax.axis_size("gy")
    k = coefficient.reshape(8, nx, ny, nz)
    ex, ey, hx, hy = nx + 3, ny + 3, nx + 2, ny + 2
    vmem = pl.BlockSpec(memory_space=pltpu.VMEM)
    smem = pl.BlockSpec(memory_space=pltpu.SMEM)
    f32 = lambda *shape: jax.ShapeDtypeStruct(shape, jnp.float32)
    bf16 = lambda *shape: jax.ShapeDtypeStruct(shape, jnp.bfloat16)

    def call(kernel, name, out_shape, args, scratch=(), limit=48, us=1, first=vmem):
        return pl.pallas_call(
            kernel,
            out_shape=out_shape,
            in_specs=[first] + [vmem] * (len(args) - 1),
            out_specs=jax.tree.map(lambda _: vmem, out_shape),
            scratch_shapes=scratch,
            compiler_params=pltpu.CompilerParams(vmem_limit_bytes=limit * 2**20),
            cost_estimate=pl.CostEstimate(flops=us * 10**9, bytes_accessed=2**20, transcendentals=0),
            name=name,
        )(*args)

    def send(v, axis, step):
        size = lax.axis_size(axis)
        pairs = [(i, i + step) for i in range(size) if 0 <= i + step < size]
        return lax.ppermute(v, axis, pairs)

    up, down = call(send_x_kernel, "send_x", (f32(8, 2, ny, nz), f32(8, 1, ny, nz)), (k,))
    xlo, xhi = send(up, "gx", 1), send(down, "gx", -1)
    up, down = call(send_y_kernel, "send_y", (f32(8, ex, 2, nz), f32(8, ex, 1, nz)), (k, xlo, xhi))
    ylo, yhi = send(up, "gy", 1), send(down, "gy", -1)
    *layers, inner = call(
        functools.partial(inner_kernel, nx, ny), "inner",
        (bf16(128, 64), f32(128, 1), bf16(2, 128, 128), f32(2, 128, 1), bf16(64, 128), f32(64, 1),
         f32((nx - 1) * (ny - 1), 64, nz)),
        (k, w_in, b_in[None], w_mid, b_mid, w_out, b_out[None]),
        scratch=[pltpu.VMEM((nx, ny, 16, nz), jnp.bfloat16)], us=7)
    side = call(
        functools.partial(side_kernel, nx, ny), "side", f32(3 * (ny - 1), 64, nz), (k, xlo, xhi, *layers),
        scratch=[pltpu.VMEM((8, 5, ny, nz), jnp.float32), pltpu.VMEM((5, ny, 16, nz), jnp.bfloat16)], us=4)
    out = call(
        functools.partial(main_kernel, nx, ny), "stencils", f32(devices * 2 * PITCH, nz),
        (owner, k, xlo, xhi, ylo, yhi, *layers, inner, side), us=12, first=smem,
        scratch=[
            pltpu.VMEM((8, ex, YP, nz), jnp.float32),
            pltpu.VMEM((8, ex, YP, nz), jnp.float32),
            pltpu.VMEM((ex, 5, 16, nz), jnp.bfloat16),
            pltpu.VMEM((ex, ey, 16, nz), jnp.float32),
            pltpu.VMEM((12, nx + 1, 24, nz), jnp.float32),
            pltpu.VMEM((3, 64 * hx * hy, nz), jnp.float32),
            pltpu.VMEM((PITCH * nx * ny, nz), jnp.float32),
            pltpu.SMEM((devices,), jnp.int32),
        ])
    got = lax.all_to_all(out.reshape(devices, -1, 4, nz), ("gx", "gy"), split_axis=0, concat_axis=0, tiled=True)
    relaid = pl.pallas_call(
        unpack_kernel,
        grid=(3,),
        out_shape=f32(27, devices * 2, nz),
        in_specs=[vmem],
        out_specs=pl.BlockSpec((9, devices * 2, nz), lambda i: (i, 0, 0)),
        compiler_params=pltpu.CompilerParams(vmem_limit_bytes=32 * 2**20),
        name="unpack",
    )(got.reshape(devices * 2 * PITCH, nz))
    return jnp.transpose(relaid, (1, 0, 2))


def solution(mesh):
    return jax.shard_map(
        per_device,
        mesh=mesh,
        in_specs=(P(None, None, None, "gx", "gy", None), P("gx", "gy"), P(), P(), P(), P(), P(), P()),
        out_specs=P(("gx", "gy"), None, None),
        check_vma=False,
    )
```

```python
import functools

import jax
import jax.numpy as jnp
from jax import lax
from jax.experimental import pallas as pl
from jax.experimental.pallas import tpu as pltpu
from jax.sharding import PartitionSpec as P

OFFSETS = [(a, b, c) for a in (-1, 0, 1) for b in (-1, 0, 1) for c in (-1, 0, 1)]
SENT = [o for o in OFFSETS if o != (0, 0, -1)]
PITCH = len(SENT)
YP = 32
UP = 24
Y0 = 8


def parity(o):
    return 4 * (o[0] != 0) + 2 * (o[1] != 0) + (o[2] != 0)


def offset_of_row(shape, dim):
    row = lax.broadcasted_iota(jnp.int32, shape, dim)
    number = jnp.zeros(shape, jnp.int32)
    none = jnp.zeros(shape, jnp.bool_)
    for lower, odd, scale in ((5, 2, 9), (4, 1, 3), (3, 0, 1)):
        low, away = (row >> lower) & 1, (row >> odd) & 1
        number += (1 + away - 2 * low) * scale
        none = jnp.logical_or(none, low > away)
    return jnp.where(none, -1, number)


def as_column(row, chosen):
    return jnp.sum(jnp.where(chosen, row, 0.0), axis=1, keepdims=True)


def z_before(v):
    lane = lax.broadcasted_iota(jnp.int32, v.shape, v.ndim - 1)
    return jnp.where(lane == 0, 0.0, pltpu.roll(v, 1, v.ndim - 1))


def z_after(v):
    lane = lax.broadcasted_iota(jnp.int32, v.shape, v.ndim - 1)
    last = v.shape[-1] - 1
    return jnp.where(lane == last, 0.0, pltpu.roll(v, last, v.ndim - 1))


def send_x_kernel(k_ref, up_ref, down_ref):
    nx = k_ref.shape[1]
    up_ref[...] = k_ref[:, nx - 2:]
    down_ref[...] = k_ref[:, :1]


def send_y_kernel(k_ref, xlo_ref, xhi_ref, up_ref, down_ref):
    nx, ny = k_ref.shape[1:3]
    for to, rows in ((up_ref, slice(ny - 2, ny)), (down_ref, slice(0, 1))):
        to[:, 0:2] = xlo_ref[:, :, rows]
        to[:, 2:2 + nx] = k_ref[:, :, rows]
        to[:, 2 + nx:] = xhi_ref[:, :, rows]


def feature_tile(kt):
    logs = jnp.log(1.0 + kt)
    return jnp.concatenate([logs, z_before(logs)], 0).astype(jnp.bfloat16)


def mlp(f, columns, layers):
    w1_ref, b1_ref, wm_ref, bm_ref, wo_ref, bo_ref = layers
    h = jnp.concatenate(
        [jnp.concatenate([f(x, y), f(x, y - 1), f(x - 1, y), f(x - 1, y - 1)], 0) for x, y in columns], 1)
    v = jnp.dot(w1_ref[...], h, preferred_element_type=jnp.float32) + b1_ref[...]
    h = (v + v * jnp.tanh(v)).astype(jnp.bfloat16)
    for m in range(2):
        v = jnp.dot(wm_ref[m], h, preferred_element_type=jnp.float32) + bm_ref[m]
        h = (v + v * jnp.tanh(v)).astype(jnp.bfloat16)
    v = jnp.dot(wo_ref[...], h, preferred_element_type=jnp.float32) + bo_ref[...]
    return 0.25 + 0.25 * jnp.tanh(v)


def inner_kernel(nx, ny, k_ref, win_ref, bin_ref, wmid_ref, bmid_ref, wout_ref, bout_ref,
                 w1_ref, b1_ref, wm_ref, bm_ref, wo_ref, bo_ref, w_ref, f_ref):
    nz = 128
    half = jnp.bfloat16(0.5)
    eye = lax.broadcasted_iota(jnp.int32, (128, 128), 0) == lax.broadcasted_iota(jnp.int32, (128, 128), 1)
    into = offset_of_row((27, 64), 1) == lax.broadcasted_iota(jnp.int32, (27, 64), 0)
    out_of = lax.broadcasted_iota(jnp.int32, (32, 27), 0) == lax.broadcasted_iota(jnp.int32, (32, 27), 1)
    ones = lambda m: jnp.where(m, 1.0, 0.0).astype(jnp.bfloat16)
    w1_ref[...] = jnp.dot(win_ref[...] * half, ones(into), preferred_element_type=jnp.float32).astype(jnp.bfloat16)
    wo_ref[...] = jnp.dot(ones(out_of), wout_ref[...] * half, preferred_element_type=jnp.float32).astype(jnp.bfloat16)
    b1_ref[...] = as_column(bin_ref[...], eye) * 0.5
    bo_ref[...] = as_column(bout_ref[...], out_of) * 0.5
    for m in range(2):
        wm_ref[m] = wmid_ref[m] * half
        bm_ref[m] = as_column(bmid_ref[m:m + 1], eye) * 0.5
    layers = (w1_ref, b1_ref, wm_ref, bm_ref, wo_ref, bo_ref)
    flat = k_ref.reshape(8 * nx * ny, nz)

    def tiles(x, _):
        for y in range(ny):
            f_ref[x, y] = feature_tile(flat[pl.ds(x * ny + y, 8, stride=nx * ny), :])
        return _

    lax.fori_loop(0, nx, tiles, 0)

    def row(x, _):
        w = mlp(lambda a, b: f_ref[a, b], [(x, y) for y in range(1, ny)], layers)
        for y in range(1, ny):
            w_ref[(x - 1) * (ny - 1) + y - 1] = w[:, (y - 1) * nz:y * nz]
        return _

    lax.fori_loop(1, nx, row, 0)


def side_kernel(nx, ny, k_ref, xlo_ref, xhi_ref, w1_ref, b1_ref, wm_ref, bm_ref, wo_ref, bo_ref, w_ref, k5_ref, f_ref):
    nz = 128
    layers = (w1_ref, b1_ref, wm_ref, bm_ref, wo_ref, bo_ref)
    k5_ref[:, 0:2] = xlo_ref[...]
    k5_ref[:, 2:3] = k_ref[:, 0:1]
    k5_ref[:, 3:4] = k_ref[:, nx - 1:]
    k5_ref[:, 4:5] = xhi_ref[...]
    flat = k5_ref.reshape(8 * 5 * ny, nz)

    def tiles(x, _):
        for y in range(ny):
            f_ref[x, y] = feature_tile(flat[pl.ds(x * ny + y, 8, stride=5 * ny), :])
        return _

    lax.fori_loop(0, 5, tiles, 0)

    def row(i, _):
        x = jnp.where(i == 2, 4, i + 1)
        w = mlp(lambda a, b: f_ref[a, b], [(x, y) for y in range(1, ny)], layers)
        for y in range(1, ny):
            w_ref[i * (ny - 1) + y - 1] = w[:, (y - 1) * nz:y * nz]
        return _

    lax.fori_loop(0, 3, row, 0)


def main_kernel(nx, ny, owner_ref, coef_ref, xlo_ref, xhi_ref, ylo_ref, yhi_ref,
                w1_ref, b1_ref, wm_ref, bm_ref, wo_ref, bo_ref, inner_ref, side_ref, out_ref,
                k_ref, r_ref, f_ref, t_ref, u_ref, s_ref, count_ref):
    nz = 128
    layers = (w1_ref, b1_ref, wm_ref, bm_ref, wo_ref, bo_ref)
    ex, ey = nx + 3, ny + 3
    hx, hy = nx + 2, ny + 2
    kp = ex * YP
    up = hx * UP
    last_x = lax.axis_index("gx") == lax.axis_size("gx") - 1
    last_y = lax.axis_index("gy") == lax.axis_size("gy") - 1

    for p in range(8):
        k_ref[p, 2:2 + nx, Y0:Y0 + ny] = coef_ref[p]
        k_ref[p, 0:2, Y0:Y0 + ny] = xlo_ref[p]
        k_ref[p, 2 + nx:, Y0:Y0 + ny] = xhi_ref[p]
        for x in range(ex):
            k_ref[p, x, Y0 - 2:Y0] = ylo_ref[p, x]
            k_ref[p, x, Y0 + ny:Y0 + ny + 1] = yhi_ref[p, x]
    flat_k = k_ref.reshape(8 * kp, nz)
    flat_r = r_ref.reshape(12 * kp, nz)

    def inverse_root(v):
        return lax.rsqrt(jnp.maximum(v, 1e-30))

    def roots(x, _):
        for p in range(8):
            for b in range(0, YP, 8):
                rows = pl.ds(pl.multiple_of(p * kp + x * YP + b, 8), 8)
                v = flat_k[rows, :]
                v = v * inverse_root(v)
                flat_r[rows, :] = v
                if p % 2:
                    flat_r[pl.ds(pl.multiple_of((8 + p // 2) * kp + x * YP + b, 8), 8), :] = z_before(v)
        return _

    lax.fori_loop(0, ex, roots, 0)

    rim = {0: 0, 1: 1, 2: 2, ey - 2: 3, ey - 1: 4}

    def tiles(x, _):
        for y, at in rim.items():
            f_ref[x, at] = feature_tile(flat_k[pl.ds(x * YP + Y0 - 2 + y, 8, stride=kp), :])
        return _

    lax.fori_loop(0, ex, tiles, 0)

    def ratios(x, _):
        for blk in range(0, ny + 1, 8):
            rows = min(8, ny + 1 - blk)

            def at(px, py, pz, dx, dy):
                p = 4 * px + 2 * py + pz
                return flat_r[pl.ds(p * kp + (x + 1 + dx) * YP + Y0 - 1 + blk + dy, rows), :]

            for p in range(8):
                px, py, pz = p >> 2, (p >> 1) & 1, p & 1
                own = flat_k[pl.ds(p * kp + (x + 1) * YP + Y0 - 1 + blk, rows), :]
                total = at(1 - px, py, pz, 0, 0) + at(1 - px, py, pz, 1 if px else -1, 0)
                total += at(px, 1 - py, pz, 0, 0) + at(px, 1 - py, pz, 0, 1 if py else -1)
                beside = at(px, py, 1 - pz, 0, 0)
                total += beside + (z_after(beside) if pz else z_before(beside))
                t = total * inverse_root(own)
                t_ref[p, x, pl.ds(blk, rows), :] = t
                if pz:
                    t_ref[8 + p // 2, x, pl.ds(blk, rows), :] = z_before(t)
        return _

    lax.fori_loop(0, nx + 1, ratios, 0)

    def put(x, y, wy):
        for n in range(0, 27, 8):
            size = min(8, 27 - n)
            u_ref[0, pl.ds(n * up + x * UP + y, size, stride=up), :] = wy[n:n + size]

    def put_inner(x, _):
        for y in range(1, ny):
            put(x + 1, y + 1, inner_ref[(x - 1) * (ny - 1) + y - 1])
        return _

    lax.fori_loop(1, nx, put_inner, 0)

    def put_side(i, _):
        for y in range(1, ny):
            put(jnp.where(i == 2, hx - 1, i), y + 1, side_ref[i * (ny - 1) + y - 1])
        return _

    lax.fori_loop(0, 3, put_side, 0)
    columns = [(x, y) for y in (0, 1, hy - 1) for x in range(hx)]
    w = mlp(lambda x, y: f_ref[x, rim[y]], [(x + 1, y + 1) for x, y in columns], layers)
    for n, (x, y) in enumerate(columns):
        put(x, y, w[:, n * nz:(n + 1) * nz])

    def scale(x, _):
        past_x = jnp.logical_and(last_x, x == hx - 1)
        for b in range(0, UP, 8):
            y = lax.broadcasted_iota(jnp.int32, (8, nz), 0) + b
            past = jnp.logical_or(past_x, jnp.logical_and(last_y, y == hy - 1))
            for n, o in enumerate(OFFSETS):
                rows = pl.ds(pl.multiple_of(n * up + x * UP + b, 8), 8)
                plane = 8 + parity(o) // 2 if o[2] == -1 else parity(o)
                r = flat_r[pl.ds(plane * kp + (x + 1 - (o[0] == -1)) * YP + Y0 - 1 + b - (o[1] == -1), 8), :]
                u = jnp.where(past, 0.0, u_ref[0, rows, :] * r)
                u_ref[0, rows, :] = u
                if o[2] != 1:
                    u_ref[1, rows, :] = z_after(u)
                if o[2] != -1:
                    u_ref[2, rows, :] = z_before(u)
        return _

    lax.fori_loop(0, hx, scale, 0)

    def galerkin(x, _):
        for yb in range(0, ny, 8):

            def u_at(f, o):
                plane = OFFSETS.index(f)
                which = {0: 0, 1: 1, -1: 2}[o[2]]
                row = plane * up + (x + 1 + o[0]) * UP + yb + 1 + o[1]
                return u_ref[which, pl.ds(row, 8), :]

            own = {f: u_at(f, (0, 0, 0)) for f in OFFSETS}
            q = {}
            for f in OFFSETS:
                p = parity(f)
                plane = 8 + p // 2 if f[2] == -1 else p
                t = t_ref[plane, x + 1 - (f[0] == -1), pl.ds(yb + 1 - (f[1] == -1), 8), :]
                total = t * own[f]
                for d in range(3):
                    for step in (-1, 1):
                        g = tuple(f[n] + (step if n == d else 0) for n in range(3))
                        if g in own:
                            total = total - own[g]
                q[f] = total
            for n, o in enumerate(SENT):
                plus = minus = None
                for fx in range(-2, 3):
                    for fy in range(-2, 3):
                        for fz in range(-2, 3):
                            f = (fx, fy, fz)
                            far = [d for d in range(3) if abs(f[d]) == 2]
                            g = tuple(f[d] - 2 * o[d] for d in range(3))
                            if len(far) > 1 or max(map(abs, g)) > 1:
                                continue
                            other = u_at(g, o)
                            if far:
                                near = tuple(v // 2 if d == far[0] else v for d, v in enumerate(f))
                                term = other * own[near]
                                minus = term if minus is None else minus + term
                            else:
                                term = other * q[f]
                                plus = term if plus is None else plus + term
                total = plus if minus is None else plus - minus
                s_ref[pl.ds(n * nx * ny + x * ny + yb, 8), :] = total
        return _

    lax.fori_loop(0, nx, galerkin, 0)

    def clear(i, _):
        rows = 2 * 2 * PITCH
        out_ref[pl.ds(pl.multiple_of(i * rows, 8), rows), :] = jnp.zeros((rows, nz), jnp.float32)
        count_ref[2 * i] = 0
        count_ref[2 * i + 1] = 0
        return _

    lax.fori_loop(0, out_ref.shape[0] // (2 * 2 * PITCH), clear, 0)

    def place(x, _):
        for y in range(ny):
            who = owner_ref[x, y]
            rank = count_ref[who]
            count_ref[who] = rank + 1
            row = (who * 2 + rank) * PITCH
            c = x * ny + y
            for n in (0, 8, 16, 24):
                size = min(8, PITCH - n)
                out_ref[pl.ds(row + n, size), :] = s_ref[pl.ds(n * nx * ny + c, size, stride=nx * ny), :]
        return _

    lax.fori_loop(0, nx, place, 0)


def unpack_kernel(in_ref, out_ref):
    group, slots = out_ref.shape[:2]
    below, above = OFFSETS.index((0, 0, -1)), SENT.index((0, 0, 1))
    first = pl.program_id(0) * group

    def one(i, _):
        o = first + i
        n = jnp.where(o > below, o - 1, o)
        for k in range(0, slots, 8):
            out_ref[i, pl.ds(k, 8), :] = in_ref[pl.ds(k * PITCH + n, 8, stride=PITCH), :]
        return _

    lax.fori_loop(0, group, one, 0)

    @pl.when(pl.program_id(0) == below // group)
    def _():
        for k in range(0, slots, 8):
            out_ref[below % group, pl.ds(k, 8), :] = z_before(in_ref[pl.ds(k * PITCH + above, 8, stride=PITCH), :])


def per_device(coefficient, owner, w_in, b_in, w_mid, b_mid, w_out, b_out):
    nx, ny, nz = coefficient.shape[3:]
    devices = lax.axis_size("gx") * lax.axis_size("gy")
    k = coefficient.reshape(8, nx, ny, nz)
    ex, ey, hx, hy = nx + 3, ny + 3, nx + 2, ny + 2
    vmem = pl.BlockSpec(memory_space=pltpu.VMEM)
    smem = pl.BlockSpec(memory_space=pltpu.SMEM)
    f32 = lambda *shape: jax.ShapeDtypeStruct(shape, jnp.float32)
    bf16 = lambda *shape: jax.ShapeDtypeStruct(shape, jnp.bfloat16)

    def call(kernel, name, out_shape, args, scratch=(), limit=32, us=1, first=vmem):
        return pl.pallas_call(
            kernel,
            out_shape=out_shape,
            in_specs=[first] + [vmem] * (len(args) - 1),
            out_specs=jax.tree.map(lambda _: vmem, out_shape),
            scratch_shapes=scratch,
            compiler_params=pltpu.CompilerParams(vmem_limit_bytes=limit * 2**20),
            cost_estimate=pl.CostEstimate(flops=us * 10**9, bytes_accessed=2**20, transcendentals=0),
            name=name,
        )(*args)

    def send(v, axis, step):
        size = lax.axis_size(axis)
        pairs = [(i, i + step) for i in range(size) if 0 <= i + step < size]
        return lax.ppermute(v, axis, pairs)

    up, down = call(send_x_kernel, "send_x", (f32(8, 2, ny, nz), f32(8, 1, ny, nz)), (k,))
    xlo, xhi = send(up, "gx", 1), send(down, "gx", -1)
    up, down = call(send_y_kernel, "send_y", (f32(8, ex, 2, nz), f32(8, ex, 1, nz)), (k, xlo, xhi))
    ylo, yhi = send(up, "gy", 1), send(down, "gy", -1)
    *layers, inner = call(
        functools.partial(inner_kernel, nx, ny), "inner",
        (bf16(128, 64), f32(128, 1), bf16(2, 128, 128), f32(2, 128, 1), bf16(32, 128), f32(32, 1),
         f32((nx - 1) * (ny - 1), 32, nz)),
        (k, w_in, b_in[None], w_mid, b_mid, w_out, b_out[None]),
        scratch=[pltpu.VMEM((nx, ny, 16, nz), jnp.bfloat16)], us=7)
    side = call(
        functools.partial(side_kernel, nx, ny), "side", f32(3 * (ny - 1), 32, nz), (k, xlo, xhi, *layers),
        scratch=[pltpu.VMEM((8, 5, ny, nz), jnp.float32), pltpu.VMEM((5, ny, 16, nz), jnp.bfloat16)], us=4)
    out = call(
        functools.partial(main_kernel, nx, ny), "stencils", f32(devices * 2 * PITCH, nz),
        (owner, k, xlo, xhi, ylo, yhi, *layers, inner, side), us=12, first=smem,
        scratch=[
            pltpu.VMEM((8, ex, YP, nz), jnp.float32),
            pltpu.VMEM((12, ex, YP, nz), jnp.float32),
            pltpu.VMEM((ex, 5, 16, nz), jnp.bfloat16),
            pltpu.VMEM((12, nx + 1, 24, nz), jnp.float32),
            pltpu.VMEM((3, 27 * hx * UP, nz), jnp.float32),
            pltpu.VMEM((PITCH * nx * ny, nz), jnp.float32),
            pltpu.SMEM((devices,), jnp.int32),
        ])
    got = lax.all_to_all(out.reshape(devices, -1, 4, nz), ("gx", "gy"), split_axis=0, concat_axis=0, tiled=True)
    relaid = pl.pallas_call(
        unpack_kernel,
        grid=(3,),
        out_shape=f32(27, devices * 2, nz),
        in_specs=[vmem],
        out_specs=pl.BlockSpec((9, devices * 2, nz), lambda i: (i, 0, 0)),
        compiler_params=pltpu.CompilerParams(vmem_limit_bytes=32 * 2**20),
        name="unpack",
    )(got.reshape(devices * 2 * PITCH, nz))
    return jnp.transpose(relaid, (1, 0, 2))


def solution(mesh):
    return jax.shard_map(
        per_device,
        mesh=mesh,
        in_specs=(P(None, None, None, "gx", "gy", None), P("gx", "gy"), P(), P(), P(), P(), P(), P()),
        out_specs=P(("gx", "gy"), None, None),
        check_vma=False,
    )
```

```python
import functools

import jax
import jax.numpy as jnp
from jax import lax
from jax.experimental import pallas as pl
from jax.experimental.pallas import tpu as pltpu
from jax.sharding import PartitionSpec as P

OFFSETS = [(a, b, c) for a in (-1, 0, 1) for b in (-1, 0, 1) for c in (-1, 0, 1)]
SENT = [o for o in OFFSETS if o != (0, 0, -1)]
PITCH = len(SENT)
YP = 24


def parity(o):
    return 4 * (o[0] != 0) + 2 * (o[1] != 0) + (o[2] != 0)


def offset_of_row(shape, dim):
    row = lax.broadcasted_iota(jnp.int32, shape, dim)
    number = jnp.zeros(shape, jnp.int32)
    none = jnp.zeros(shape, jnp.bool_)
    for lower, odd, scale in ((5, 2, 9), (4, 1, 3), (3, 0, 1)):
        low, away = (row >> lower) & 1, (row >> odd) & 1
        number += (1 + away - 2 * low) * scale
        none = jnp.logical_or(none, low > away)
    return jnp.where(none, -1, number)


def as_column(row, chosen):
    return jnp.sum(jnp.where(chosen, row, 0.0), axis=1, keepdims=True)


def z_before(v):
    lane = lax.broadcasted_iota(jnp.int32, v.shape, v.ndim - 1)
    return jnp.where(lane == 0, 0.0, pltpu.roll(v, 1, v.ndim - 1))


def z_after(v):
    lane = lax.broadcasted_iota(jnp.int32, v.shape, v.ndim - 1)
    last = v.shape[-1] - 1
    return jnp.where(lane == last, 0.0, pltpu.roll(v, last, v.ndim - 1))


def send_x_kernel(k_ref, up_ref, down_ref):
    nx = k_ref.shape[1]
    up_ref[...] = k_ref[:, nx - 2:]
    down_ref[...] = k_ref[:, :1]


def send_y_kernel(k_ref, xlo_ref, xhi_ref, up_ref, down_ref):
    nx, ny = k_ref.shape[1:3]
    for to, rows in ((up_ref, slice(ny - 2, ny)), (down_ref, slice(0, 1))):
        to[:, 0:2] = xlo_ref[:, :, rows]
        to[:, 2:2 + nx] = k_ref[:, :, rows]
        to[:, 2 + nx:] = xhi_ref[:, :, rows]


def feature_tile(kt):
    logs = jnp.log(1.0 + kt)
    return jnp.concatenate([logs, z_before(logs)], 0).astype(jnp.bfloat16)


def mlp(f, columns, layers):
    w1_ref, b1_ref, wm_ref, bm_ref, wo_ref, bo_ref = layers
    h = jnp.concatenate(
        [jnp.concatenate([f(x, y), f(x, y - 1), f(x - 1, y), f(x - 1, y - 1)], 0) for x, y in columns], 1)
    v = jnp.dot(w1_ref[...], h, preferred_element_type=jnp.float32) + b1_ref[...]
    h = (v + v * jnp.tanh(v)).astype(jnp.bfloat16)
    for m in range(2):
        v = jnp.dot(wm_ref[m], h, preferred_element_type=jnp.float32) + bm_ref[m]
        h = (v + v * jnp.tanh(v)).astype(jnp.bfloat16)
    v = jnp.dot(wo_ref[...], h, preferred_element_type=jnp.float32) + bo_ref[...]
    return 0.25 + 0.25 * jnp.tanh(v)


def inner_kernel(nx, ny, k_ref, win_ref, bin_ref, wmid_ref, bmid_ref, wout_ref, bout_ref,
                 w1_ref, b1_ref, wm_ref, bm_ref, wo_ref, bo_ref, w_ref, f_ref):
    nz = 128
    half = jnp.bfloat16(0.5)
    eye = lax.broadcasted_iota(jnp.int32, (128, 128), 0) == lax.broadcasted_iota(jnp.int32, (128, 128), 1)
    into = offset_of_row((27, 64), 1) == lax.broadcasted_iota(jnp.int32, (27, 64), 0)
    out_of = lax.broadcasted_iota(jnp.int32, (32, 27), 0) == lax.broadcasted_iota(jnp.int32, (32, 27), 1)
    ones = lambda m: jnp.where(m, 1.0, 0.0).astype(jnp.bfloat16)
    w1_ref[...] = jnp.dot(win_ref[...] * half, ones(into), preferred_element_type=jnp.float32).astype(jnp.bfloat16)
    wo_ref[...] = jnp.dot(ones(out_of), wout_ref[...] * half, preferred_element_type=jnp.float32).astype(jnp.bfloat16)
    b1_ref[...] = as_column(bin_ref[...], eye) * 0.5
    bo_ref[...] = as_column(bout_ref[...], out_of) * 0.5
    for m in range(2):
        wm_ref[m] = wmid_ref[m] * half
        bm_ref[m] = as_column(bmid_ref[m:m + 1], eye) * 0.5
    layers = (w1_ref, b1_ref, wm_ref, bm_ref, wo_ref, bo_ref)
    flat = k_ref.reshape(8 * nx * ny, nz)

    def tiles(x):
        for y in range(ny):
            f_ref[x, y] = feature_tile(flat[pl.ds(x * ny + y, 8, stride=nx * ny), :])

    tiles(0)
    tiles(1)

    def row(x, _):
        w = mlp(lambda a, b: f_ref[a, b], [(x, y) for y in range(1, ny)], layers)
        tiles(jnp.minimum(x + 1, nx - 1))
        for y in range(1, ny):
            w_ref[(x - 1) * (ny - 1) + y - 1] = w[:, (y - 1) * nz:y * nz]
        return _

    lax.fori_loop(1, nx, row, 0)


def side_kernel(nx, ny, k_ref, xlo_ref, xhi_ref, w1_ref, b1_ref, wm_ref, bm_ref, wo_ref, bo_ref, w_ref, k5_ref, f_ref):
    nz = 128
    layers = (w1_ref, b1_ref, wm_ref, bm_ref, wo_ref, bo_ref)
    k5_ref[:, 0:2] = xlo_ref[...]
    k5_ref[:, 2:3] = k_ref[:, 0:1]
    k5_ref[:, 3:4] = k_ref[:, nx - 1:]
    k5_ref[:, 4:5] = xhi_ref[...]
    flat = k5_ref.reshape(8 * 5 * ny, nz)

    def tiles(x, _):
        for y in range(ny):
            f_ref[x, y] = feature_tile(flat[pl.ds(x * ny + y, 8, stride=5 * ny), :])
        return _

    lax.fori_loop(0, 5, tiles, 0)

    def row(i, _):
        x = jnp.where(i == 2, 4, i + 1)
        w = mlp(lambda a, b: f_ref[a, b], [(x, y) for y in range(1, ny)], layers)
        for y in range(1, ny):
            w_ref[i * (ny - 1) + y - 1] = w[:, (y - 1) * nz:y * nz]
        return _

    lax.fori_loop(0, 3, row, 0)


def main_kernel(nx, ny, owner_ref, coef_ref, xlo_ref, xhi_ref, ylo_ref, yhi_ref,
                w1_ref, b1_ref, wm_ref, bm_ref, wo_ref, bo_ref, inner_ref, side_ref, out_ref,
                k_ref, r_ref, f_ref, t_ref, u_ref, keep_ref, s_ref, slot_ref, count_ref):
    nz = 128
    layers = (w1_ref, b1_ref, wm_ref, bm_ref, wo_ref, bo_ref)
    ex, ey = nx + 3, ny + 3
    hx, hy = nx + 2, ny + 2
    kp = r_ref.shape[0] // 12
    tp = t_ref.shape[0] // 12
    up = (hx + 1) * YP
    last_x = lax.axis_index("gx") == lax.axis_size("gx") - 1
    last_y = lax.axis_index("gy") == lax.axis_size("gy") - 1

    for p in range(8):
        for x in range(ex):
            row = p * kp + (x + 1) * YP
            if x < 2:
                own = xlo_ref[p, x]
            elif x < 2 + nx:
                own = coef_ref[p, x - 2]
            else:
                own = xhi_ref[p, x - 2 - nx]
            k_ref[row - 2:row] = ylo_ref[p, x]
            k_ref[row:row + ny] = own
            k_ref[row + ny:row + ny + 1] = yhi_ref[p, x]

    def inverse_root(v):
        return lax.rsqrt(jnp.maximum(v, 1e-30))

    def roots(i, _):
        for p in range(8):
            rows = pl.ds(pl.multiple_of(p * kp + 8 * i, 8), 8)
            v = k_ref[rows, :]
            v = v * inverse_root(v)
            r_ref[rows, :] = v
            if p % 2:
                r_ref[pl.ds(pl.multiple_of((8 + p // 2) * kp + 8 * i, 8), 8), :] = z_before(v)
        return _

    lax.fori_loop(0, kp // 8, roots, 0, unroll=6)

    def ratios(i, _):
        def at(px, py, pz, dx, dy):
            p = 4 * px + 2 * py + pz
            return r_ref[pl.ds(p * kp + 8 * i + YP + YP * dx + dy, 8), :]

        for p in range(8):
            px, py, pz = p >> 2, (p >> 1) & 1, p & 1
            own = k_ref[pl.ds(pl.multiple_of(p * kp + 8 * i + YP, 8), 8), :]
            total = at(1 - px, py, pz, 0, 0) + at(1 - px, py, pz, 1 if px else -1, 0)
            total += at(px, 1 - py, pz, 0, 0) + at(px, 1 - py, pz, 0, 1 if py else -1)
            beside = at(px, py, 1 - pz, 0, 0)
            total += beside + (z_after(beside) if pz else z_before(beside))
            t = total * inverse_root(own)
            t_ref[pl.ds(pl.multiple_of(p * tp + 8 * i, 8), 8), :] = t
            if pz:
                t_ref[pl.ds(pl.multiple_of((8 + p // 2) * tp + 8 * i, 8), 8), :] = z_before(t)
        return _

    lax.fori_loop(0, tp // 8, ratios, 0, unroll=5)

    def put(x, y, wy):
        for n in range(0, 27, 8):
            size = min(8, 27 - n)
            u_ref[0, pl.ds(n * up + (x + 1) * YP + y - 1, size, stride=up), :] = wy[n:n + size]

    def put_inner(x, _):
        for y in range(1, ny):
            put(x + 1, y + 1, inner_ref[(x - 1) * (ny - 1) + y - 1])
        return _

    lax.fori_loop(1, nx, put_inner, 0)

    def put_side(i, _):
        for y in range(1, ny):
            put(jnp.where(i == 2, hx - 1, i), y + 1, side_ref[i * (ny - 1) + y - 1])
        return _

    lax.fori_loop(0, 3, put_side, 0)
    rim = {0: 0, 1: 1, 2: 2, ey - 2: 3, ey - 1: 4}
    for x in range(ex):
        for y, at in rim.items():
            f_ref[x, at] = feature_tile(k_ref[pl.ds((x + 1) * YP + y - 2, 8, stride=kp), :])
    columns = [(x, y) for y in (0, 1, hy - 1) for x in range(hx)]
    w = mlp(lambda x, y: f_ref[x, rim[y]], [(x + 1, y + 1) for x, y in columns], layers)
    out_ref[...] = jnp.zeros(out_ref.shape, jnp.float32)
    for n, (x, y) in enumerate(columns):
        put(x, y, w[:, n * nz:(n + 1) * nz])

    row = lax.broadcasted_iota(jnp.int32, (up, nz), 0)
    keep_ref[...] = jnp.where(jnp.logical_and(last_x, row >= hx * YP - 1), 0.0, 1.0)

    @pl.when(last_y)
    def _():
        for x in range(hx):
            keep_ref[(x + 1) * YP + ny:(x + 1) * YP + ny + 1] = jnp.zeros((1, nz), jnp.float32)

    def scale(i, _):
        keep = keep_ref[pl.ds(pl.multiple_of(8 * i, 8), 8), :]
        rows = [pl.ds(pl.multiple_of(n * up + 8 * i, 8), 8) for n in range(27)]
        scaled = []
        for n, o in enumerate(OFFSETS):
            plane = 8 + parity(o) // 2 if o[2] == -1 else parity(o)
            at = plane * kp + 8 * i + (0 if o[0] == -1 else YP) + (-1 if o[1] == -1 else 0)
            scaled.append(u_ref[0, rows[n], :] * (r_ref[pl.ds(at, 8), :] * keep))
        for n, o in enumerate(OFFSETS):
            u_ref[0, rows[n], :] = scaled[n]
            if o[2] != 1:
                u_ref[1, rows[n], :] = z_after(scaled[n])
            if o[2] != -1:
                u_ref[2, rows[n], :] = z_before(scaled[n])
        return _

    lax.fori_loop(0, up // 8, scale, 0, unroll=3)

    for who in range(count_ref.shape[0]):
        count_ref[who] = 0

    def place(x):
        for y in range(ny):
            row = slot_ref[x, y]
            c = x * ny + y
            for n in range(0, PITCH, 8):
                size = min(8, PITCH - n)
                out_ref[pl.ds(row + n, size), :] = s_ref[pl.ds(n * nx * ny + c, size, stride=nx * ny), :]

    def galerkin(x, _):
        for y in range(ny):
            who = owner_ref[x, y]
            rank = count_ref[who]
            count_ref[who] = rank + 1
            slot_ref[x, y] = (who * 2 + rank) * PITCH
        for yb in range(0, ny, 8):

            def u_at(f, o):
                plane = OFFSETS.index(f)
                which = {0: 0, 1: 1, -1: 2}[o[2]]
                row = plane * up + (x + 2 + o[0]) * YP + yb + o[1]
                return u_ref[which, pl.ds(row, 8), :]

            own = {f: u_at(f, (0, 0, 0)) for f in OFFSETS}
            q = {}
            for f in OFFSETS:
                p = parity(f)
                plane = 8 + p // 2 if f[2] == -1 else p
                t = t_ref[pl.ds(plane * tp + (x + 2 - (f[0] == -1)) * YP + yb - (f[1] == -1), 8), :]
                total = t * own[f]
                for d in range(3):
                    for step in (-1, 1):
                        g = tuple(f[n] + (step if n == d else 0) for n in range(3))
                        if g in own:
                            total = total - own[g]
                q[f] = total
            for n, o in enumerate(SENT):
                plus = minus = None
                for fx in range(-2, 3):
                    for fy in range(-2, 3):
                        for fz in range(-2, 3):
                            f = (fx, fy, fz)
                            far = [d for d in range(3) if abs(f[d]) == 2]
                            g = tuple(f[d] - 2 * o[d] for d in range(3))
                            if len(far) > 1 or max(map(abs, g)) > 1:
                                continue
                            other = u_at(g, o)
                            if far:
                                near = tuple(v // 2 if d == far[0] else v for d, v in enumerate(f))
                                term = other * own[near]
                                minus = term if minus is None else minus + term
                            else:
                                term = other * q[f]
                                plus = term if plus is None else plus + term
                total = plus if minus is None else plus - minus
                s_ref[pl.ds(n * nx * ny + x * ny + yb, 8), :] = total
        return _

    lax.fori_loop(0, nx, galerkin, 0)

    lax.fori_loop(0, nx, lambda x, _: (place(x), _)[1], 0)


def unpack_kernel(in_ref, out_ref):
    group, slots = out_ref.shape[:2]
    below, above = OFFSETS.index((0, 0, -1)), SENT.index((0, 0, 1))
    first = pl.program_id(0) * group

    def one(i, _):
        o = first + i
        n = jnp.where(o > below, o - 1, o)
        for k in range(0, slots, 8):
            out_ref[i, pl.ds(k, 8), :] = in_ref[pl.ds(k * PITCH + n, 8, stride=PITCH), :]
        return _

    lax.fori_loop(0, group, one, 0)

    @pl.when(pl.program_id(0) == below // group)
    def _():
        for k in range(0, slots, 8):
            out_ref[below % group, pl.ds(k, 8), :] = z_before(in_ref[pl.ds(k * PITCH + above, 8, stride=PITCH), :])


def per_device(coefficient, owner, w_in, b_in, w_mid, b_mid, w_out, b_out):
    nx, ny, nz = coefficient.shape[3:]
    devices = lax.axis_size("gx") * lax.axis_size("gy")
    k = coefficient.reshape(8, nx, ny, nz)
    ex, ey, hx, hy = nx + 3, ny + 3, nx + 2, ny + 2
    fine, ratio = (ex + 1) * YP, (nx + 2) * YP
    vmem = pl.BlockSpec(memory_space=pltpu.VMEM)
    smem = pl.BlockSpec(memory_space=pltpu.SMEM)
    f32 = lambda *shape: jax.ShapeDtypeStruct(shape, jnp.float32)
    bf16 = lambda *shape: jax.ShapeDtypeStruct(shape, jnp.bfloat16)

    def call(kernel, name, out_shape, args, scratch=(), limit=32, us=1, first=vmem):
        return pl.pallas_call(
            kernel,
            out_shape=out_shape,
            in_specs=[first] + [vmem] * (len(args) - 1),
            out_specs=jax.tree.map(lambda _: vmem, out_shape),
            scratch_shapes=scratch,
            compiler_params=pltpu.CompilerParams(vmem_limit_bytes=limit * 2**20),
            cost_estimate=pl.CostEstimate(flops=us * 10**9, bytes_accessed=2**20, transcendentals=0),
            name=name,
        )(*args)

    def send(v, axis, step):
        size = lax.axis_size(axis)
        pairs = [(i, i + step) for i in range(size) if 0 <= i + step < size]
        return lax.ppermute(v, axis, pairs)

    up, down = call(send_x_kernel, "send_x", (f32(8, 2, ny, nz), f32(8, 1, ny, nz)), (k,))
    xlo, xhi = send(up, "gx", 1), send(down, "gx", -1)
    up, down = call(send_y_kernel, "send_y", (f32(8, ex, 2, nz), f32(8, ex, 1, nz)), (k, xlo, xhi))
    ylo, yhi = send(up, "gy", 1), send(down, "gy", -1)
    *layers, inner = call(
        functools.partial(inner_kernel, nx, ny), "inner",
        (bf16(128, 64), f32(128, 1), bf16(2, 128, 128), f32(2, 128, 1), bf16(32, 128), f32(32, 1),
         f32((nx - 1) * (ny - 1), 32, nz)),
        (k, w_in, b_in[None], w_mid, b_mid, w_out, b_out[None]),
        scratch=[pltpu.VMEM((nx, ny, 16, nz), jnp.bfloat16)], us=7)
    side = call(
        functools.partial(side_kernel, nx, ny), "side", f32(3 * (ny - 1), 32, nz), (k, xlo, xhi, *layers),
        scratch=[pltpu.VMEM((8, 5, ny, nz), jnp.float32), pltpu.VMEM((5, ny, 16, nz), jnp.bfloat16)], us=4)
    out = call(
        functools.partial(main_kernel, nx, ny), "stencils", f32(devices * 2 * PITCH, nz),
        (owner, k, xlo, xhi, ylo, yhi, *layers, inner, side), us=12, first=smem,
        scratch=[
            pltpu.VMEM((8 * fine, nz), jnp.float32),
            pltpu.VMEM((12 * fine, nz), jnp.float32),
            pltpu.VMEM((ex, 5, 16, nz), jnp.bfloat16),
            pltpu.VMEM((12 * ratio, nz), jnp.float32),
            pltpu.VMEM((3, 27 * (hx + 1) * YP, nz), jnp.float32),
            pltpu.VMEM(((hx + 1) * YP, nz), jnp.float32),
            pltpu.VMEM((PITCH * nx * ny, nz), jnp.float32),
            pltpu.SMEM((nx, ny), jnp.int32),
            pltpu.SMEM((devices,), jnp.int32),
        ])
    got = lax.all_to_all(out.reshape(devices, -1, 4, nz), ("gx", "gy"), split_axis=0, concat_axis=0, tiled=True)
    relaid = pl.pallas_call(
        unpack_kernel,
        grid=(3,),
        out_shape=f32(27, devices * 2, nz),
        in_specs=[vmem],
        out_specs=pl.BlockSpec((9, devices * 2, nz), lambda i: (i, 0, 0)),
        compiler_params=pltpu.CompilerParams(vmem_limit_bytes=32 * 2**20),
        name="unpack",
    )(got.reshape(devices * 2 * PITCH, nz))
    return jnp.transpose(relaid, (1, 0, 2))


def solution(mesh):
    return jax.shard_map(
        per_device,
        mesh=mesh,
        in_specs=(P(None, None, None, "gx", "gy", None), P("gx", "gy"), P(), P(), P(), P(), P(), P()),
        out_specs=P(("gx", "gy"), None, None),
        check_vma=False,
    )
```

```python
import functools

import jax
import jax.numpy as jnp
from jax import lax
from jax.experimental import pallas as pl
from jax.experimental.pallas import tpu as pltpu
from jax.sharding import PartitionSpec as P

OFFSETS = [(a, b, c) for a in (-1, 0, 1) for b in (-1, 0, 1) for c in (-1, 0, 1)]
SENT = [o for o in OFFSETS if o != (0, 0, -1)]
PITCH = len(SENT)
YP = 24


def parity(o):
    return 4 * (o[0] != 0) + 2 * (o[1] != 0) + (o[2] != 0)


def offset_of_row(shape, dim):
    row = lax.broadcasted_iota(jnp.int32, shape, dim)
    number = jnp.zeros(shape, jnp.int32)
    none = jnp.zeros(shape, jnp.bool_)
    for lower, odd, scale in ((5, 2, 9), (4, 1, 3), (3, 0, 1)):
        low, away = (row >> lower) & 1, (row >> odd) & 1
        number += (1 + away - 2 * low) * scale
        none = jnp.logical_or(none, low > away)
    return jnp.where(none, -1, number)


def as_column(row, chosen):
    return jnp.sum(jnp.where(chosen, row, 0.0), axis=1, keepdims=True)


def z_before(v):
    lane = lax.broadcasted_iota(jnp.int32, v.shape, v.ndim - 1)
    return jnp.where(lane == 0, 0.0, pltpu.roll(v, 1, v.ndim - 1))


def z_after(v):
    lane = lax.broadcasted_iota(jnp.int32, v.shape, v.ndim - 1)
    last = v.shape[-1] - 1
    return jnp.where(lane == last, 0.0, pltpu.roll(v, last, v.ndim - 1))


def send_x_kernel(k_ref, up_ref, down_ref):
    nx = k_ref.shape[1]
    up_ref[...] = k_ref[:, nx - 2:]
    down_ref[...] = k_ref[:, :1]


def send_y_kernel(k_ref, xlo_ref, xhi_ref, up_ref, down_ref):
    nx, ny = k_ref.shape[1:3]
    for to, rows in ((up_ref, slice(ny - 2, ny)), (down_ref, slice(0, 1))):
        to[:, 0:2] = xlo_ref[:, :, rows]
        to[:, 2:2 + nx] = k_ref[:, :, rows]
        to[:, 2 + nx:] = xhi_ref[:, :, rows]


def feature_tile(kt):
    logs = jnp.log(1.0 + kt)
    return jnp.concatenate([logs, z_before(logs)], 0).astype(jnp.bfloat16)


def mlp(f, columns, layers):
    w1_ref, b1_ref, wm_ref, bm_ref, wo_ref, bo_ref = layers
    h = jnp.concatenate(
        [jnp.concatenate([f(x, y), f(x, y - 1), f(x - 1, y), f(x - 1, y - 1)], 0) for x, y in columns], 1)
    v = jnp.dot(w1_ref[...], h, preferred_element_type=jnp.float32) + b1_ref[...]
    h = (v + v * jnp.tanh(v)).astype(jnp.bfloat16)
    for m in range(2):
        v = jnp.dot(wm_ref[m], h, preferred_element_type=jnp.float32) + bm_ref[m]
        h = (v + v * jnp.tanh(v)).astype(jnp.bfloat16)
    v = jnp.dot(wo_ref[...], h, preferred_element_type=jnp.float32) + bo_ref[...]
    return 0.25 + 0.25 * jnp.tanh(v)


def inner_kernel(nx, ny, k_ref, win_ref, bin_ref, wmid_ref, bmid_ref, wout_ref, bout_ref,
                 w1_ref, b1_ref, wm_ref, bm_ref, wo_ref, bo_ref, w_ref, f_ref):
    nz = 128
    half = jnp.bfloat16(0.5)
    eye = lax.broadcasted_iota(jnp.int32, (128, 128), 0) == lax.broadcasted_iota(jnp.int32, (128, 128), 1)
    into = offset_of_row((27, 64), 1) == lax.broadcasted_iota(jnp.int32, (27, 64), 0)
    out_of = lax.broadcasted_iota(jnp.int32, (32, 27), 0) == lax.broadcasted_iota(jnp.int32, (32, 27), 1)
    ones = lambda m: jnp.where(m, 1.0, 0.0).astype(jnp.bfloat16)
    w1_ref[...] = jnp.dot(win_ref[...] * half, ones(into), preferred_element_type=jnp.float32).astype(jnp.bfloat16)
    wo_ref[...] = jnp.dot(ones(out_of), wout_ref[...] * half, preferred_element_type=jnp.float32).astype(jnp.bfloat16)
    b1_ref[...] = as_column(bin_ref[...], eye) * 0.5
    bo_ref[...] = as_column(bout_ref[...], out_of) * 0.5
    for m in range(2):
        wm_ref[m] = wmid_ref[m] * half
        bm_ref[m] = as_column(bmid_ref[m:m + 1], eye) * 0.5
    layers = (w1_ref, b1_ref, wm_ref, bm_ref, wo_ref, bo_ref)
    flat = k_ref.reshape(8 * nx * ny, nz)

    def tiles(x):
        for y in range(ny):
            f_ref[x, y] = feature_tile(flat[pl.ds(x * ny + y, 8, stride=nx * ny), :])

    tiles(0)
    tiles(1)

    def row(x, _):
        w = mlp(lambda a, b: f_ref[a, b], [(x, y) for y in range(1, ny)], layers)
        tiles(jnp.minimum(x + 1, nx - 1))
        for y in range(1, ny):
            w_ref[(x - 1) * (ny - 1) + y - 1] = w[:, (y - 1) * nz:y * nz]
        return _

    lax.fori_loop(1, nx, row, 0, unroll=True)


def side_kernel(nx, ny, k_ref, xlo_ref, xhi_ref, w1_ref, b1_ref, wm_ref, bm_ref, wo_ref, bo_ref, w_ref, k5_ref, f_ref):
    nz = 128
    layers = (w1_ref, b1_ref, wm_ref, bm_ref, wo_ref, bo_ref)
    k5_ref[:, 0:2] = xlo_ref[...]
    k5_ref[:, 2:3] = k_ref[:, 0:1]
    k5_ref[:, 3:4] = k_ref[:, nx - 1:]
    k5_ref[:, 4:5] = xhi_ref[...]
    flat = k5_ref.reshape(8 * 5 * ny, nz)

    def tiles(x, _):
        for y in range(ny):
            f_ref[x, y] = feature_tile(flat[pl.ds(x * ny + y, 8, stride=5 * ny), :])
        return _

    lax.fori_loop(0, 5, tiles, 0, unroll=True)

    def row(i, _):
        x = jnp.where(i == 2, 4, i + 1)
        w = mlp(lambda a, b: f_ref[a, b], [(x, y) for y in range(1, ny)], layers)
        for y in range(1, ny):
            w_ref[i * (ny - 1) + y - 1] = w[:, (y - 1) * nz:y * nz]
        return _

    lax.fori_loop(0, 3, row, 0, unroll=True)


def main_kernel(nx, ny, owner_ref, coef_ref, xlo_ref, xhi_ref, ylo_ref, yhi_ref,
                w1_ref, b1_ref, wm_ref, bm_ref, wo_ref, bo_ref, inner_ref, side_ref, out_ref,
                k_ref, r_ref, f_ref, t_ref, u_ref, keep_ref, s_ref, slot_ref, count_ref):
    nz = 128
    layers = (w1_ref, b1_ref, wm_ref, bm_ref, wo_ref, bo_ref)
    ex, ey = nx + 3, ny + 3
    hx, hy = nx + 2, ny + 2
    kp = r_ref.shape[0] // 12
    tp = t_ref.shape[0] // 12
    up = (hx + 1) * YP
    last_x = lax.axis_index("gx") == lax.axis_size("gx") - 1
    last_y = lax.axis_index("gy") == lax.axis_size("gy") - 1

    for p in range(8):
        for x in range(ex):
            row = p * kp + (x + 1) * YP
            if x < 2:
                own = xlo_ref[p, x]
            elif x < 2 + nx:
                own = coef_ref[p, x - 2]
            else:
                own = xhi_ref[p, x - 2 - nx]
            k_ref[row - 2:row] = ylo_ref[p, x]
            k_ref[row:row + ny] = own
            k_ref[row + ny:row + ny + 1] = yhi_ref[p, x]

    def inverse_root(v):
        return lax.rsqrt(jnp.maximum(v, 1e-30))

    def roots(i, _):
        for p in range(8):
            rows = pl.ds(pl.multiple_of(p * kp + 8 * i, 8), 8)
            v = k_ref[rows, :]
            v = v * inverse_root(v)
            r_ref[rows, :] = v
            if p % 2:
                r_ref[pl.ds(pl.multiple_of((8 + p // 2) * kp + 8 * i, 8), 8), :] = z_before(v)
        return _

    lax.fori_loop(0, kp // 8, roots, 0, unroll=12)

    def ratios(i, _):
        def at(px, py, pz, dx, dy):
            p = 4 * px + 2 * py + pz
            return r_ref[pl.ds(p * kp + 8 * i + YP + YP * dx + dy, 8), :]

        for p in range(8):
            px, py, pz = p >> 2, (p >> 1) & 1, p & 1
            own = k_ref[pl.ds(pl.multiple_of(p * kp + 8 * i + YP, 8), 8), :]
            total = at(1 - px, py, pz, 0, 0) + at(1 - px, py, pz, 1 if px else -1, 0)
            total += at(px, 1 - py, pz, 0, 0) + at(px, 1 - py, pz, 0, 1 if py else -1)
            beside = at(px, py, 1 - pz, 0, 0)
            total += beside + (z_after(beside) if pz else z_before(beside))
            t = total * inverse_root(own)
            t_ref[pl.ds(pl.multiple_of(p * tp + 8 * i, 8), 8), :] = t
            if pz:
                t_ref[pl.ds(pl.multiple_of((8 + p // 2) * tp + 8 * i, 8), 8), :] = z_before(t)
        return _

    lax.fori_loop(0, tp // 8, ratios, 0, unroll=10)

    def put(x, y, wy):
        for n in range(0, 27, 8):
            size = min(8, 27 - n)
            u_ref[0, pl.ds(n * up + (x + 1) * YP + y - 1, size, stride=up), :] = wy[n:n + size]

    def put_inner(x, _):
        for y in range(1, ny):
            put(x + 1, y + 1, inner_ref[(x - 1) * (ny - 1) + y - 1])
        return _

    lax.fori_loop(1, nx, put_inner, 0)

    def put_side(i, _):
        for y in range(1, ny):
            put(jnp.where(i == 2, hx - 1, i), y + 1, side_ref[i * (ny - 1) + y - 1])
        return _

    lax.fori_loop(0, 3, put_side, 0)
    rim = {0: 0, 1: 1, 2: 2, ey - 2: 3, ey - 1: 4}
    for x in range(ex):
        for y, at in rim.items():
            f_ref[x, at] = feature_tile(k_ref[pl.ds((x + 1) * YP + y - 2, 8, stride=kp), :])
    columns = [(x, y) for y in (0, 1, hy - 1) for x in range(hx)]
    w = mlp(lambda x, y: f_ref[x, rim[y]], [(x + 1, y + 1) for x, y in columns], layers)
    out_ref[...] = jnp.zeros(out_ref.shape, jnp.float32)
    for n, (x, y) in enumerate(columns):
        put(x, y, w[:, n * nz:(n + 1) * nz])

    row = lax.broadcasted_iota(jnp.int32, (up, nz), 0)
    keep_ref[...] = jnp.where(jnp.logical_and(last_x, row >= hx * YP - 1), 0.0, 1.0)

    @pl.when(last_y)
    def _():
        for x in range(hx):
            keep_ref[(x + 1) * YP + ny:(x + 1) * YP + ny + 1] = jnp.zeros((1, nz), jnp.float32)

    def scale(i, _):
        keep = keep_ref[pl.ds(pl.multiple_of(8 * i, 8), 8), :]
        rows = [pl.ds(pl.multiple_of(n * up + 8 * i, 8), 8) for n in range(27)]
        scaled = []
        for n, o in enumerate(OFFSETS):
            plane = 8 + parity(o) // 2 if o[2] == -1 else parity(o)
            at = plane * kp + 8 * i + (0 if o[0] == -1 else YP) + (-1 if o[1] == -1 else 0)
            scaled.append(u_ref[0, rows[n], :] * (r_ref[pl.ds(at, 8), :] * keep))
        for n, o in enumerate(OFFSETS):
            u_ref[0, rows[n], :] = scaled[n]
            if o[2] != 1:
                u_ref[1, rows[n], :] = z_after(scaled[n])
            if o[2] != -1:
                u_ref[2, rows[n], :] = z_before(scaled[n])
        return _

    lax.fori_loop(0, up // 8, scale, 0, unroll=11)

    for who in range(count_ref.shape[0]):
        count_ref[who] = 0

    def place(x):
        for y in range(ny):
            row = slot_ref[x, y]
            c = x * ny + y
            for n in range(0, PITCH, 8):
                size = min(8, PITCH - n)
                out_ref[pl.ds(row + n, size), :] = s_ref[pl.ds(n * nx * ny + c, size, stride=nx * ny), :]

    def galerkin(x, _):
        for y in range(ny):
            who = owner_ref[x, y]
            rank = count_ref[who]
            count_ref[who] = rank + 1
            slot_ref[x, y] = (who * 2 + rank) * PITCH
        for yb in range(0, ny, 8):

            def u_at(f, o):
                plane = OFFSETS.index(f)
                which = {0: 0, 1: 1, -1: 2}[o[2]]
                row = plane * up + (x + 2 + o[0]) * YP + yb + o[1]
                return u_ref[which, pl.ds(row, 8), :]

            own = {f: u_at(f, (0, 0, 0)) for f in OFFSETS}
            q = {}
            for f in OFFSETS:
                p = parity(f)
                plane = 8 + p // 2 if f[2] == -1 else p
                t = t_ref[pl.ds(plane * tp + (x + 2 - (f[0] == -1)) * YP + yb - (f[1] == -1), 8), :]
                total = t * own[f]
                for d in range(3):
                    for step in (-1, 1):
                        g = tuple(f[n] + (step if n == d else 0) for n in range(3))
                        if g in own:
                            total = total - own[g]
                q[f] = total
            for n, o in enumerate(SENT):
                plus = minus = None
                for fx in range(-2, 3):
                    for fy in range(-2, 3):
                        for fz in range(-2, 3):
                            f = (fx, fy, fz)
                            far = [d for d in range(3) if abs(f[d]) == 2]
                            g = tuple(f[d] - 2 * o[d] for d in range(3))
                            if len(far) > 1 or max(map(abs, g)) > 1:
                                continue
                            other = u_at(g, o)
                            if far:
                                near = tuple(v // 2 if d == far[0] else v for d, v in enumerate(f))
                                term = other * own[near]
                                minus = term if minus is None else minus + term
                            else:
                                term = other * q[f]
                                plus = term if plus is None else plus + term
                total = plus if minus is None else plus - minus
                s_ref[pl.ds(n * nx * ny + x * ny + yb, 8), :] = total
        return _

    lax.fori_loop(0, nx, galerkin, 0, unroll=2)

    lax.fori_loop(0, nx, lambda x, _: (place(x), _)[1], 0)


def unpack_kernel(in_ref, out_ref):
    group, slots = out_ref.shape[:2]
    below, above = OFFSETS.index((0, 0, -1)), SENT.index((0, 0, 1))
    first = pl.program_id(0) * group

    def one(i, _):
        o = first + i
        n = jnp.where(o > below, o - 1, o)
        for k in range(0, slots, 8):
            out_ref[i, pl.ds(k, 8), :] = in_ref[pl.ds(k * PITCH + n, 8, stride=PITCH), :]
        return _

    lax.fori_loop(0, group, one, 0)

    @pl.when(pl.program_id(0) == below // group)
    def _():
        for k in range(0, slots, 8):
            out_ref[below % group, pl.ds(k, 8), :] = z_before(in_ref[pl.ds(k * PITCH + above, 8, stride=PITCH), :])


def per_device(coefficient, owner, w_in, b_in, w_mid, b_mid, w_out, b_out):
    nx, ny, nz = coefficient.shape[3:]
    devices = lax.axis_size("gx") * lax.axis_size("gy")
    k = coefficient.reshape(8, nx, ny, nz)
    ex, ey, hx, hy = nx + 3, ny + 3, nx + 2, ny + 2
    fine, ratio = (ex + 1) * YP, (nx + 2) * YP
    vmem = pl.BlockSpec(memory_space=pltpu.VMEM)
    smem = pl.BlockSpec(memory_space=pltpu.SMEM)
    f32 = lambda *shape: jax.ShapeDtypeStruct(shape, jnp.float32)
    bf16 = lambda *shape: jax.ShapeDtypeStruct(shape, jnp.bfloat16)

    def call(kernel, name, out_shape, args, scratch=(), limit=32, us=1, first=vmem):
        return pl.pallas_call(
            kernel,
            out_shape=out_shape,
            in_specs=[first] + [vmem] * (len(args) - 1),
            out_specs=jax.tree.map(lambda _: vmem, out_shape),
            scratch_shapes=scratch,
            compiler_params=pltpu.CompilerParams(vmem_limit_bytes=limit * 2**20),
            cost_estimate=pl.CostEstimate(flops=us * 10**9, bytes_accessed=2**20, transcendentals=0),
            name=name,
        )(*args)

    def send(v, axis, step):
        size = lax.axis_size(axis)
        pairs = [(i, i + step) for i in range(size) if 0 <= i + step < size]
        return lax.ppermute(v, axis, pairs)

    up, down = call(send_x_kernel, "send_x", (f32(8, 2, ny, nz), f32(8, 1, ny, nz)), (k,))
    xlo, xhi = send(up, "gx", 1), send(down, "gx", -1)
    up, down = call(send_y_kernel, "send_y", (f32(8, ex, 2, nz), f32(8, ex, 1, nz)), (k, xlo, xhi))
    ylo, yhi = send(up, "gy", 1), send(down, "gy", -1)
    *layers, inner = call(
        functools.partial(inner_kernel, nx, ny), "inner",
        (bf16(128, 64), f32(128, 1), bf16(2, 128, 128), f32(2, 128, 1), bf16(32, 128), f32(32, 1),
         f32((nx - 1) * (ny - 1), 32, nz)),
        (k, w_in, b_in[None], w_mid, b_mid, w_out, b_out[None]),
        scratch=[pltpu.VMEM((nx, ny, 16, nz), jnp.bfloat16)], us=7)
    side = call(
        functools.partial(side_kernel, nx, ny), "side", f32(3 * (ny - 1), 32, nz), (k, xlo, xhi, *layers),
        scratch=[pltpu.VMEM((8, 5, ny, nz), jnp.float32), pltpu.VMEM((5, ny, 16, nz), jnp.bfloat16)], us=4)
    out = call(
        functools.partial(main_kernel, nx, ny), "stencils", f32(devices * 2 * PITCH, nz),
        (owner, k, xlo, xhi, ylo, yhi, *layers, inner, side), us=12, first=smem,
        scratch=[
            pltpu.VMEM((8 * fine, nz), jnp.float32),
            pltpu.VMEM((12 * fine, nz), jnp.float32),
            pltpu.VMEM((ex, 5, 16, nz), jnp.bfloat16),
            pltpu.VMEM((12 * ratio, nz), jnp.float32),
            pltpu.VMEM((3, 27 * (hx + 1) * YP, nz), jnp.float32),
            pltpu.VMEM(((hx + 1) * YP, nz), jnp.float32),
            pltpu.VMEM((PITCH * nx * ny, nz), jnp.float32),
            pltpu.SMEM((nx, ny), jnp.int32),
            pltpu.SMEM((devices,), jnp.int32),
        ])
    got = lax.all_to_all(out.reshape(devices, -1, 4, nz), ("gx", "gy"), split_axis=0, concat_axis=0, tiled=True)
    relaid = pl.pallas_call(
        unpack_kernel,
        grid=(3,),
        out_shape=f32(27, devices * 2, nz),
        in_specs=[vmem],
        out_specs=pl.BlockSpec((9, devices * 2, nz), lambda i: (i, 0, 0)),
        compiler_params=pltpu.CompilerParams(vmem_limit_bytes=32 * 2**20),
        name="unpack",
    )(got.reshape(devices * 2 * PITCH, nz))
    return jnp.transpose(relaid, (1, 0, 2))


def solution(mesh):
    return jax.shard_map(
        per_device,
        mesh=mesh,
        in_specs=(P(None, None, None, "gx", "gy", None), P("gx", "gy"), P(), P(), P(), P(), P(), P()),
        out_specs=P(("gx", "gy"), None, None),
        check_vma=False,
    )
```

```python
import functools

import jax
import jax.numpy as jnp
from jax import lax
from jax.experimental import pallas as pl
from jax.experimental.pallas import tpu as pltpu
from jax.sharding import PartitionSpec as P

OFFSETS = [(a, b, c) for a in (-1, 0, 1) for b in (-1, 0, 1) for c in (-1, 0, 1)]
SENT = [o for o in OFFSETS if o != (0, 0, -1)]
PITCH = len(SENT)
YP = 24


def parity(o):
    return 4 * (o[0] != 0) + 2 * (o[1] != 0) + (o[2] != 0)


def offset_of_row(shape, dim):
    row = lax.broadcasted_iota(jnp.int32, shape, dim)
    number = jnp.zeros(shape, jnp.int32)
    none = jnp.zeros(shape, jnp.bool_)
    for lower, odd, scale in ((5, 2, 9), (4, 1, 3), (3, 0, 1)):
        low, away = (row >> lower) & 1, (row >> odd) & 1
        number += (1 + away - 2 * low) * scale
        none = jnp.logical_or(none, low > away)
    return jnp.where(none, -1, number)


def as_column(row, chosen):
    return jnp.sum(jnp.where(chosen, row, 0.0), axis=1, keepdims=True)


def z_before(v):
    lane = lax.broadcasted_iota(jnp.int32, v.shape, v.ndim - 1)
    return jnp.where(lane == 0, 0.0, pltpu.roll(v, 1, v.ndim - 1))


def z_after(v):
    lane = lax.broadcasted_iota(jnp.int32, v.shape, v.ndim - 1)
    last = v.shape[-1] - 1
    return jnp.where(lane == last, 0.0, pltpu.roll(v, last, v.ndim - 1))


def send_x_kernel(k_ref, up_ref, down_ref):
    nx = k_ref.shape[1]
    up_ref[...] = k_ref[:, nx - 2:]
    down_ref[...] = k_ref[:, :1]


def send_y_kernel(k_ref, xlo_ref, xhi_ref, up_ref, down_ref):
    nx, ny = k_ref.shape[1:3]
    for to, rows in ((up_ref, slice(ny - 2, ny)), (down_ref, slice(0, 1))):
        to[:, 0:2] = xlo_ref[:, :, rows]
        to[:, 2:2 + nx] = k_ref[:, :, rows]
        to[:, 2 + nx:] = xhi_ref[:, :, rows]


def feature_tile(kt):
    logs = jnp.log(1.0 + kt)
    return jnp.concatenate([logs, z_before(logs)], 0).astype(jnp.bfloat16)


def mlp(f, columns, layers):
    w1_ref, b1_ref, wm_ref, bm_ref, wo_ref, bo_ref = layers
    h = jnp.concatenate(
        [jnp.concatenate([f(x, y), f(x, y - 1), f(x - 1, y), f(x - 1, y - 1)], 0) for x, y in columns], 1)
    v = jnp.dot(w1_ref[...], h, preferred_element_type=jnp.float32) + b1_ref[...]
    h = (v + v * jnp.tanh(v)).astype(jnp.bfloat16)
    for m in range(2):
        v = jnp.dot(wm_ref[m], h, preferred_element_type=jnp.float32) + bm_ref[m]
        h = (v + v * jnp.tanh(v)).astype(jnp.bfloat16)
    v = jnp.dot(wo_ref[...], h, preferred_element_type=jnp.float32) + bo_ref[...]
    return 0.25 + 0.25 * jnp.tanh(v)


def inner_kernel(nx, ny, k_ref, win_ref, bin_ref, wmid_ref, bmid_ref, wout_ref, bout_ref,
                 w1_ref, b1_ref, wm_ref, bm_ref, wo_ref, bo_ref, w_ref, f_ref):
    nz = 128
    half = jnp.bfloat16(0.5)
    eye = lax.broadcasted_iota(jnp.int32, (128, 128), 0) == lax.broadcasted_iota(jnp.int32, (128, 128), 1)
    into = offset_of_row((27, 64), 1) == lax.broadcasted_iota(jnp.int32, (27, 64), 0)
    out_of = lax.broadcasted_iota(jnp.int32, (32, 27), 0) == lax.broadcasted_iota(jnp.int32, (32, 27), 1)
    ones = lambda m: jnp.where(m, 1.0, 0.0).astype(jnp.bfloat16)
    w1_ref[...] = jnp.dot(win_ref[...] * half, ones(into), preferred_element_type=jnp.float32).astype(jnp.bfloat16)
    wo_ref[...] = jnp.dot(ones(out_of), wout_ref[...] * half, preferred_element_type=jnp.float32).astype(jnp.bfloat16)
    b1_ref[...] = as_column(bin_ref[...], eye) * 0.5
    bo_ref[...] = as_column(bout_ref[...], out_of) * 0.5
    for m in range(2):
        wm_ref[m] = wmid_ref[m] * half
        bm_ref[m] = as_column(bmid_ref[m:m + 1], eye) * 0.5
    layers = (w1_ref, b1_ref, wm_ref, bm_ref, wo_ref, bo_ref)
    flat = k_ref.reshape(8 * nx * ny, nz)

    def tiles(x):
        for y in range(ny):
            f_ref[x, y] = feature_tile(flat[pl.ds(x * ny + y, 8, stride=nx * ny), :])

    tiles(0)
    tiles(1)

    def row(x, _):
        w = mlp(lambda a, b: f_ref[a, b], [(x, y) for y in range(1, ny)], layers)
        tiles(jnp.minimum(x + 1, nx - 1))
        for y in range(1, ny):
            w_ref[(x - 1) * (ny - 1) + y - 1] = w[:, (y - 1) * nz:y * nz]
        return _

    lax.fori_loop(1, nx, row, 0, unroll=True)


def side_kernel(nx, ny, k_ref, xlo_ref, xhi_ref, w1_ref, b1_ref, wm_ref, bm_ref, wo_ref, bo_ref, w_ref, k5_ref, f_ref):
    nz = 128
    layers = (w1_ref, b1_ref, wm_ref, bm_ref, wo_ref, bo_ref)
    k5_ref[:, 0:2] = xlo_ref[...]
    k5_ref[:, 2:3] = k_ref[:, 0:1]
    k5_ref[:, 3:4] = k_ref[:, nx - 1:]
    k5_ref[:, 4:5] = xhi_ref[...]
    flat = k5_ref.reshape(8 * 5 * ny, nz)

    def tiles(x, _):
        for y in range(ny):
            f_ref[x, y] = feature_tile(flat[pl.ds(x * ny + y, 8, stride=5 * ny), :])
        return _

    lax.fori_loop(0, 5, tiles, 0, unroll=True)

    def row(i, _):
        x = jnp.where(i == 2, 4, i + 1)
        w = mlp(lambda a, b: f_ref[a, b], [(x, y) for y in range(1, ny)], layers)
        for y in range(1, ny):
            w_ref[i * (ny - 1) + y - 1] = w[:, (y - 1) * nz:y * nz]
        return _

    lax.fori_loop(0, 3, row, 0, unroll=True)


def main_kernel(nx, ny, owner_ref, coef_ref, xlo_ref, xhi_ref, ylo_ref, yhi_ref,
                w1_ref, b1_ref, wm_ref, bm_ref, wo_ref, bo_ref, inner_ref, side_ref, out_ref,
                k_ref, r_ref, f_ref, t_ref, u_ref, keep_ref, s_ref, slot_ref, count_ref):
    nz = 128
    layers = (w1_ref, b1_ref, wm_ref, bm_ref, wo_ref, bo_ref)
    ex, ey = nx + 3, ny + 3
    hx, hy = nx + 2, ny + 2
    kp = r_ref.shape[0] // 12
    tp = t_ref.shape[0] // 12
    up = (hx + 1) * YP
    last_x = lax.axis_index("gx") == lax.axis_size("gx") - 1
    last_y = lax.axis_index("gy") == lax.axis_size("gy") - 1

    for p in range(8):
        for x in range(ex):
            row = p * kp + (x + 1) * YP
            if x < 2:
                own = xlo_ref[p, x]
            elif x < 2 + nx:
                own = coef_ref[p, x - 2]
            else:
                own = xhi_ref[p, x - 2 - nx]
            k_ref[row - 2:row] = ylo_ref[p, x]
            k_ref[row:row + ny] = own
            k_ref[row + ny:row + ny + 1] = yhi_ref[p, x]

    def inverse_root(v):
        return lax.rsqrt(jnp.maximum(v, 1e-30))

    def roots(i, _):
        for p in range(8):
            rows = pl.ds(pl.multiple_of(p * kp + 8 * i, 8), 8)
            v = k_ref[rows, :]
            v = v * inverse_root(v)
            r_ref[rows, :] = v
            if p % 2:
                r_ref[pl.ds(pl.multiple_of((8 + p // 2) * kp + 8 * i, 8), 8), :] = z_before(v)
        return _

    lax.fori_loop(0, kp // 8, roots, 0, unroll=12)

    def ratios(i, _):
        def at(px, py, pz, dx, dy):
            p = 4 * px + 2 * py + pz
            return r_ref[pl.ds(p * kp + 8 * i + YP + YP * dx + dy, 8), :]

        for p in range(8):
            px, py, pz = p >> 2, (p >> 1) & 1, p & 1
            own = k_ref[pl.ds(pl.multiple_of(p * kp + 8 * i + YP, 8), 8), :]
            total = at(1 - px, py, pz, 0, 0) + at(1 - px, py, pz, 1 if px else -1, 0)
            total += at(px, 1 - py, pz, 0, 0) + at(px, 1 - py, pz, 0, 1 if py else -1)
            beside = at(px, py, 1 - pz, 0, 0)
            total += beside + (z_after(beside) if pz else z_before(beside))
            t = total * inverse_root(own)
            t_ref[pl.ds(pl.multiple_of(p * tp + 8 * i, 8), 8), :] = t
            if pz:
                t_ref[pl.ds(pl.multiple_of((8 + p // 2) * tp + 8 * i, 8), 8), :] = z_before(t)
        return _

    lax.fori_loop(0, tp // 8, ratios, 0, unroll=10)

    def put(x, y, wy):
        for n in range(0, 27, 8):
            size = min(8, 27 - n)
            u_ref[0, pl.ds(n * up + (x + 1) * YP + y - 1, size, stride=up), :] = wy[n:n + size]

    def put_inner(x, _):
        for y in range(1, ny):
            put(x + 1, y + 1, inner_ref[(x - 1) * (ny - 1) + y - 1])
        return _

    lax.fori_loop(1, nx, put_inner, 0)

    def put_side(i, _):
        for y in range(1, ny):
            put(jnp.where(i == 2, hx - 1, i), y + 1, side_ref[i * (ny - 1) + y - 1])
        return _

    lax.fori_loop(0, 3, put_side, 0)
    rim = {0: 0, 1: 1, 2: 2, ey - 2: 3, ey - 1: 4}
    for x in range(ex):
        for y, at in rim.items():
            f_ref[x, at] = feature_tile(k_ref[pl.ds((x + 1) * YP + y - 2, 8, stride=kp), :])
    columns = [(x, y) for y in (0, 1, hy - 1) for x in range(hx)]
    w = mlp(lambda x, y: f_ref[x, rim[y]], [(x + 1, y + 1) for x, y in columns], layers)
    out_ref[...] = jnp.zeros(out_ref.shape, jnp.float32)
    for n, (x, y) in enumerate(columns):
        put(x, y, w[:, n * nz:(n + 1) * nz])

    row = lax.broadcasted_iota(jnp.int32, (up, nz), 0)
    keep_ref[...] = jnp.where(jnp.logical_and(last_x, row >= hx * YP - 1), 0.0, 1.0)

    @pl.when(last_y)
    def _():
        for x in range(hx):
            keep_ref[(x + 1) * YP + ny:(x + 1) * YP + ny + 1] = jnp.zeros((1, nz), jnp.float32)

    def scale(i, _):
        keep = keep_ref[pl.ds(pl.multiple_of(8 * i, 8), 8), :]
        rows = [pl.ds(pl.multiple_of(n * up + 8 * i, 8), 8) for n in range(27)]
        scaled = []
        for n, o in enumerate(OFFSETS):
            plane = 8 + parity(o) // 2 if o[2] == -1 else parity(o)
            at = plane * kp + 8 * i + (0 if o[0] == -1 else YP) + (-1 if o[1] == -1 else 0)
            scaled.append(u_ref[0, rows[n], :] * (r_ref[pl.ds(at, 8), :] * keep))
        for n, o in enumerate(OFFSETS):
            u_ref[0, rows[n], :] = scaled[n]
            if o[2] != 1:
                u_ref[1, rows[n], :] = z_after(scaled[n])
            if o[2] != -1:
                u_ref[2, rows[n], :] = z_before(scaled[n])
        return _

    lax.fori_loop(0, up // 8, scale, 0, unroll=11)

    for who in range(count_ref.shape[0]):
        count_ref[who] = 0

    def place(x):
        for y in range(ny):
            row = slot_ref[x, y]
            c = x * ny + y
            for n in range(0, PITCH, 8):
                size = min(8, PITCH - n)
                out_ref[pl.ds(row + n, size), :] = s_ref[pl.ds(n * nx * ny + c, size, stride=nx * ny), :]

    def galerkin(x, _):
        for y in range(ny):
            who = owner_ref[x, y]
            rank = count_ref[who]
            count_ref[who] = rank + 1
            slot_ref[x, y] = (who * 2 + rank) * PITCH
        for yb in range(0, ny, 8):

            def u_at(f, o):
                plane = OFFSETS.index(f)
                which = {0: 0, 1: 1, -1: 2}[o[2]]
                row = plane * up + (x + 2 + o[0]) * YP + yb + o[1]
                return u_ref[which, pl.ds(row, 8), :]

            own = {f: u_at(f, (0, 0, 0)) for f in OFFSETS}
            q = {}
            for f in OFFSETS:
                p = parity(f)
                plane = 8 + p // 2 if f[2] == -1 else p
                t = t_ref[pl.ds(plane * tp + (x + 2 - (f[0] == -1)) * YP + yb - (f[1] == -1), 8), :]
                total = t * own[f]
                for d in range(3):
                    for step in (-1, 1):
                        g = tuple(f[n] + (step if n == d else 0) for n in range(3))
                        if g in own:
                            total = total - own[g]
                q[f] = total
            for n, o in enumerate(SENT):
                plus = minus = None
                for fx in range(-2, 3):
                    for fy in range(-2, 3):
                        for fz in range(-2, 3):
                            f = (fx, fy, fz)
                            far = [d for d in range(3) if abs(f[d]) == 2]
                            g = tuple(f[d] - 2 * o[d] for d in range(3))
                            if len(far) > 1 or max(map(abs, g)) > 1:
                                continue
                            other = u_at(g, o)
                            if far:
                                near = tuple(v // 2 if d == far[0] else v for d, v in enumerate(f))
                                term = other * own[near]
                                minus = term if minus is None else minus + term
                            else:
                                term = other * q[f]
                                plus = term if plus is None else plus + term
                total = plus if minus is None else plus - minus
                s_ref[pl.ds(n * nx * ny + x * ny + yb, 8), :] = total
        return _

    lax.fori_loop(0, nx, galerkin, 0, unroll=4)

    lax.fori_loop(0, nx, lambda x, _: (place(x), _)[1], 0)


def unpack_kernel(in_ref, out_ref):
    group, slots = out_ref.shape[:2]
    below, above = OFFSETS.index((0, 0, -1)), SENT.index((0, 0, 1))
    first = pl.program_id(0) * group

    def one(i, _):
        o = first + i
        n = jnp.where(o > below, o - 1, o)
        for k in range(0, slots, 8):
            out_ref[i, pl.ds(k, 8), :] = in_ref[pl.ds(k * PITCH + n, 8, stride=PITCH), :]
        return _

    lax.fori_loop(0, group, one, 0, unroll=3)

    @pl.when(pl.program_id(0) == below // group)
    def _():
        for k in range(0, slots, 8):
            out_ref[below % group, pl.ds(k, 8), :] = z_before(in_ref[pl.ds(k * PITCH + above, 8, stride=PITCH), :])


def per_device(coefficient, owner, w_in, b_in, w_mid, b_mid, w_out, b_out):
    nx, ny, nz = coefficient.shape[3:]
    devices = lax.axis_size("gx") * lax.axis_size("gy")
    k = coefficient.reshape(8, nx, ny, nz)
    ex, ey, hx, hy = nx + 3, ny + 3, nx + 2, ny + 2
    fine, ratio = (ex + 1) * YP, (nx + 2) * YP
    vmem = pl.BlockSpec(memory_space=pltpu.VMEM)
    smem = pl.BlockSpec(memory_space=pltpu.SMEM)
    f32 = lambda *shape: jax.ShapeDtypeStruct(shape, jnp.float32)
    bf16 = lambda *shape: jax.ShapeDtypeStruct(shape, jnp.bfloat16)

    def call(kernel, name, out_shape, args, scratch=(), limit=32, us=1, first=vmem):
        return pl.pallas_call(
            kernel,
            out_shape=out_shape,
            in_specs=[first] + [vmem] * (len(args) - 1),
            out_specs=jax.tree.map(lambda _: vmem, out_shape),
            scratch_shapes=scratch,
            compiler_params=pltpu.CompilerParams(vmem_limit_bytes=limit * 2**20),
            cost_estimate=pl.CostEstimate(flops=us * 10**9, bytes_accessed=2**20, transcendentals=0),
            name=name,
        )(*args)

    def send(v, axis, step):
        size = lax.axis_size(axis)
        pairs = [(i, i + step) for i in range(size) if 0 <= i + step < size]
        return lax.ppermute(v, axis, pairs)

    up, down = call(send_x_kernel, "send_x", (f32(8, 2, ny, nz), f32(8, 1, ny, nz)), (k,))
    xlo, xhi = send(up, "gx", 1), send(down, "gx", -1)
    up, down = call(send_y_kernel, "send_y", (f32(8, ex, 2, nz), f32(8, ex, 1, nz)), (k, xlo, xhi))
    ylo, yhi = send(up, "gy", 1), send(down, "gy", -1)
    *layers, inner = call(
        functools.partial(inner_kernel, nx, ny), "inner",
        (bf16(128, 64), f32(128, 1), bf16(2, 128, 128), f32(2, 128, 1), bf16(32, 128), f32(32, 1),
         f32((nx - 1) * (ny - 1), 32, nz)),
        (k, w_in, b_in[None], w_mid, b_mid, w_out, b_out[None]),
        scratch=[pltpu.VMEM((nx, ny, 16, nz), jnp.bfloat16)], us=7)
    side = call(
        functools.partial(side_kernel, nx, ny), "side", f32(3 * (ny - 1), 32, nz), (k, xlo, xhi, *layers),
        scratch=[pltpu.VMEM((8, 5, ny, nz), jnp.float32), pltpu.VMEM((5, ny, 16, nz), jnp.bfloat16)], us=4)
    out = call(
        functools.partial(main_kernel, nx, ny), "stencils", f32(devices * 2 * PITCH, nz),
        (owner, k, xlo, xhi, ylo, yhi, *layers, inner, side), us=12, first=smem,
        scratch=[
            pltpu.VMEM((8 * fine, nz), jnp.float32),
            pltpu.VMEM((12 * fine, nz), jnp.float32),
            pltpu.VMEM((ex, 5, 16, nz), jnp.bfloat16),
            pltpu.VMEM((12 * ratio, nz), jnp.float32),
            pltpu.VMEM((3, 27 * (hx + 1) * YP, nz), jnp.float32),
            pltpu.VMEM(((hx + 1) * YP, nz), jnp.float32),
            pltpu.VMEM((PITCH * nx * ny, nz), jnp.float32),
            pltpu.SMEM((nx, ny), jnp.int32),
            pltpu.SMEM((devices,), jnp.int32),
        ])
    got = lax.all_to_all(out.reshape(devices, -1, 4, nz), ("gx", "gy"), split_axis=0, concat_axis=0, tiled=True)
    relaid = pl.pallas_call(
        unpack_kernel,
        grid=(3,),
        out_shape=f32(27, devices * 2, nz),
        in_specs=[vmem],
        out_specs=pl.BlockSpec((9, devices * 2, nz), lambda i: (i, 0, 0)),
        compiler_params=pltpu.CompilerParams(vmem_limit_bytes=32 * 2**20),
        name="unpack",
    )(got.reshape(devices * 2 * PITCH, nz))
    return jnp.transpose(relaid, (1, 0, 2))


def solution(mesh):
    return jax.shard_map(
        per_device,
        mesh=mesh,
        in_specs=(P(None, None, None, "gx", "gy", None), P("gx", "gy"), P(), P(), P(), P(), P(), P()),
        out_specs=P(("gx", "gy"), None, None),
        check_vma=False,
    )
```
